128 devices in a mesh: nz: 4 (over y_hi, core), nx: 32 (over z, y_lo, x).
Axes of the slice: x: 4, y: 4 (y_hi: 2, y_lo: 2; y = y_hi * 2 + y_lo), z: 4, core: 2. Of those that a mesh axis runs over, the one named last changes fastest.
Arguments:
- phi_hat: bfloat16 [344, 704, 513], P('nz', 'nx'), may hold values from -6 to 6
- vel_hat: bfloat16 [344, 704, 513], P('nz', 'nx'), may hold values from -6 to 6
- helm_basis: bfloat16 [513, 513], replicated, may hold values from -0.25 to 0.25
- helm_dual: bfloat16 [513, 513], replicated, may hold values from -0.25 to 0.25
- helm_rates: float32 [513], replicated, may hold values from 0.5 to 20
Outputs:
- phi_new: float32 [344, 704, 513], P('nz', 'nx')
The draws below stay inside these ranges and needn't reach their ends.
All inputs are finite; a program needn't handle non-finite values.
Results may differ from the reference program's by a relative error of at most 0.035.
Values may be sent and summed in bfloat16 or wider, within the bound.
A program may use at most 128 MiB of HBM per device.

```python
import math
import jax
import jax.numpy as jnp
from jax import lax

NX = 1024
NZ = 512
MX = 704
MZ = 344
NY = 513


def shard_levels(stream_key, dims, cuts, low, top_value):
    level, own = 1.0, jax.random.fold_in(stream_key, 6)
    for position, blocks in cuts:
        heights = jnp.exp(jax.random.uniform(jax.random.fold_in(own, position), (blocks,), jnp.float32, low / len(cuts), top_value / len(cuts)))
        level = level * jnp.repeat(heights, dims[position] // blocks).reshape([-1 if axis == position else 1 for axis in range(len(dims))])
    return level


def noise(rng, dims, scale, reach, split=(), kind=jnp.bfloat16):
    factor_of = shard_levels(rng, dims, split, -0.22, 0.18) if split else 1.0
    drawn = jax.random.normal(rng, dims, jnp.float32) * scale * factor_of
    return jnp.minimum(jnp.maximum(drawn, -reach), reach).astype(kind)


def setup_inputs(seed: int = 0) -> dict:
    splits = jax.random.split(jax.random.key(seed), 6)
    return {
        "phi_hat": noise(splits[0], (MZ, MX, NY), 0.7, 6.0, ((0, 4), (1, 32))),
        "vel_hat": noise(splits[1], (MZ, MX, NY), 1.0, 6.0, ((0, 4), (1, 32))),
        "helm_basis": noise(splits[2], (NY, NY), NY ** -0.5, 0.25),
        "helm_dual": noise(splits[3], (NY, NY), NY ** -0.5, 0.25),
        "helm_rates": jnp.clip(jnp.exp(jax.random.uniform(splits[4], (NY,), jnp.float32, math.log(0.5), math.log(20.0))), 0.5, 20.0),
    }


mobility = 1.0
capillary = 0.2
screen_low = 4.0
screen_high = 20.0
time_step = 1.0 / (screen_low * screen_high * mobility * capillary)
stabilizer = capillary * (screen_low + screen_high)

def fourier_tables(mode_count, point_count):
    half_count = mode_count // 2
    mode_index = jnp.arange(mode_count, dtype=jnp.int32)
    point_index = jnp.arange(point_count, dtype=jnp.int32)
    wave_index = jnp.where(mode_index < half_count, mode_index, mode_index - half_count + 1)
    phase_steps = wave_index[:, None] * point_index[None, :] % point_count
    angles = phase_steps.astype(jnp.float32) * (2.0 * math.pi / point_count)
    basis = jnp.where((mode_index < half_count)[:, None], jnp.cos(angles), jnp.sin(angles))
    factor = math.sqrt(2.0 / mode_count)
    synthesis = (factor * basis).astype(jnp.bfloat16)
    weights = jnp.where(mode_index == 0, 1.0, 2.0).astype(jnp.float32) / (point_count * factor)
    analysis = (basis.T * weights[None, :]).astype(jnp.bfloat16)
    wavenumber = 2.0 * wave_index.astype(jnp.float32) / half_count
    return (synthesis, analysis, wavenumber)

def chebyshev_tables(count):
    index = jnp.arange(count, dtype=jnp.int32)
    period = 2 * (count - 1)
    phase_steps = index[:, None] * index[None, :] % period
    cosines = jnp.cos(phase_steps.astype(jnp.float32) * (math.pi / (count - 1)))
    factor = math.sqrt(2.0 / count)
    synthesis = (factor * cosines).astype(jnp.bfloat16)
    ends = jnp.where((index == 0) | (index == count - 1), 2.0, 1.0).astype(jnp.float32)
    analysis = (cosines.T * (2.0 / ((count - 1) * factor)) / (ends[:, None] * ends[None, :])).astype(jnp.bfloat16)
    upper = index[:, None]
    lower = index[None, :]
    deriv = jnp.where((upper > lower) & ((upper + lower) % 2 == 1), 2.0 * upper.astype(jnp.float32) / ends[None, :], 0.0)
    return (synthesis, analysis, deriv.astype(jnp.bfloat16))

def reference(phi_hat, vel_hat, helm_basis, helm_dual, helm_rates):
    synth_x, analy_x, wave_x = fourier_tables(MX, NX)
    synth_z, analy_z, wave_z = fourier_tables(MZ, NZ)
    synth_y, analy_y, deriv_y = chebyshev_tables(NY)
    table_y = synth_y.astype(jnp.float32)
    phi_rows = jnp.einsum('kmn,nj->jkm', phi_hat.astype(jnp.float32), table_y).astype(jnp.bfloat16)
    vel_rows = jnp.einsum('kmn,nj->jkm', vel_hat.astype(jnp.float32), table_y).astype(jnp.bfloat16)

    def plane(pieces):
        phi_plane, vel_plane = pieces
        phi_span = jnp.dot(synth_z.T, phi_plane, preferred_element_type=jnp.float32).astype(jnp.bfloat16)
        vel_span = jnp.dot(synth_z.T, vel_plane, preferred_element_type=jnp.float32).astype(jnp.bfloat16)
        phi_phys = jnp.dot(phi_span, synth_x, preferred_element_type=jnp.float32)
        vel_phys = jnp.dot(vel_span, synth_x, preferred_element_type=jnp.float32)
        cube = (phi_phys * phi_phys * phi_phys).astype(jnp.bfloat16)
        flux = (vel_phys * phi_phys).astype(jnp.bfloat16)

        def back(field):
            partial_x = jnp.dot(field, analy_x, preferred_element_type=jnp.float32).astype(jnp.bfloat16)
            return jnp.dot(analy_z.T, partial_x, preferred_element_type=jnp.float32).astype(jnp.bfloat16)
        return (back(cube), back(flux))
    cube_rows, flux_rows = lax.map(plane, (phi_rows, vel_rows))
    cube_cols = jnp.transpose(cube_rows, (1, 0, 2))
    flux_cols = jnp.transpose(flux_rows, (1, 0, 2))
    eigen = -helm_rates

    def solve(pieces):
        phi_row, cube_col, flux_col, wave_span = pieces
        cube_spec = jnp.dot(cube_col.T, analy_y, preferred_element_type=jnp.float32)
        flux_spec = jnp.dot(flux_col.T, analy_y, preferred_element_type=jnp.float32)
        squares = (wave_span * wave_span + wave_x * wave_x)[:, None]
        phi_float = phi_row.astype(jnp.float32)
        source = (cube_spec - (1.0 + stabilizer) * phi_float).astype(jnp.bfloat16)
        slope = jnp.dot(flux_spec.astype(jnp.bfloat16), deriv_y, preferred_element_type=jnp.float32)
        lifted = jnp.dot(source, helm_dual.T, preferred_element_type=jnp.float32)
        scaled = ((eigen[None, :] - squares) * lifted).astype(jnp.bfloat16)
        lap_part = jnp.dot(scaled, helm_basis.T, preferred_element_type=jnp.float32)
        forcing = ((phi_float / time_step + mobility * lap_part - 8.0 / (NY - 1) * slope) / (capillary * mobility)).astype(jnp.bfloat16)
        first = (jnp.dot(forcing, helm_dual.T, preferred_element_type=jnp.float32) / (eigen[None, :] - squares - screen_low)).astype(jnp.bfloat16)
        middle = jnp.dot(first, helm_basis.T, preferred_element_type=jnp.float32).astype(jnp.bfloat16)
        second = (jnp.dot(middle, helm_dual.T, preferred_element_type=jnp.float32) / (eigen[None, :] - squares - screen_high)).astype(jnp.bfloat16)
        return jnp.dot(second, helm_basis.T, preferred_element_type=jnp.float32)
    return lax.map(solve, (phi_hat, cube_cols, flux_cols, wave_z))
```

```python
import math

import jax
import jax.numpy as jnp
import ml_dtypes
import numpy as np
from jax import lax
from jax.experimental import pallas as pl
from jax.experimental.pallas import tpu as pltpu
from jax.sharding import PartitionSpec as P

NX = 1024
NZ = 512

mobility = 1.0
capillary = 0.2
screen_low = 4.0
screen_high = 20.0
time_step = 1.0 / (screen_low * screen_high * mobility * capillary)
stabilizer = capillary * (screen_low + screen_high)

PLANES = 4
HALVES = 2
WINDOW = 88
LANES = 1024
TILE = 128
BF = ml_dtypes.bfloat16
F32 = jnp.float32
BF16 = jnp.bfloat16


def fourier_tables(mode_count, point_count):
    half_count = mode_count // 2
    mode_index = np.arange(mode_count)
    wave_index = np.where(mode_index < half_count, mode_index, mode_index - half_count + 1)
    phase_steps = wave_index[:, None] * np.arange(point_count)[None, :] % point_count
    angles = phase_steps * (2.0 * math.pi / point_count)
    basis = np.where((mode_index < half_count)[:, None], np.cos(angles), np.sin(angles))
    factor = math.sqrt(2.0 / mode_count)
    weights = np.where(mode_index == 0, 1.0, 2.0) / (point_count * factor)
    wavenumber = 2.0 * wave_index / half_count
    return (
        (factor * basis).astype(np.float32).astype(BF),
        (basis.T * weights[None, :]).astype(np.float32).astype(BF),
        wavenumber.astype(np.float32),
    )


def chebyshev_tables(count):
    index = np.arange(count)
    phase_steps = index[:, None] * index[None, :] % (2 * (count - 1))
    cosines = np.cos(phase_steps * (math.pi / (count - 1)))
    factor = math.sqrt(2.0 / count)
    ends = np.where((index == 0) | (index == count - 1), 2.0, 1.0)
    analysis = cosines.T * (2.0 / ((count - 1) * factor)) / (ends[:, None] * ends[None, :])
    upper, lower = index[:, None], index[None, :]
    deriv = np.where((upper > lower) & ((upper + lower) % 2 == 1), 2.0 * upper / ends[None, :], 0.0)
    as_bf = lambda t: t.astype(np.float32).astype(BF)
    return as_bf(factor * cosines), as_bf(analysis), as_bf(deriv)


def dot(left, right):
    return jnp.dot(left, right, preferred_element_type=F32)


def dot_nt(left, right):
    return lax.dot_general(left, right, (((1,), (1,)), ((), ())), preferred_element_type=F32)


def dot_tn(left, right):
    return lax.dot_general(left, right, (((0,), (0,)), ((), ())), preferred_element_type=F32)


def rows_of(shape, axis):
    return lax.broadcasted_iota(jnp.int32, shape, axis)


MESH = pl.DeviceIdType.MESH
DEVICES = 128
BLOCK = 256
WIDE = 512


class Place:
    def __init__(self):
        self.a, self.b = lax.axis_index("nz"), lax.axis_index("nx")
        self.me = self.a * 32 + self.b
        self.core = lax.rem(self.a, 2)
        self.y = (self.a // 2) * 2 + lax.rem(self.b // 4, 2)
        self.z, self.x = self.b // 8, lax.rem(self.b, 4)

    def at(self, dz, dy, dx, dc):
        z, y, x = lax.rem(self.z + dz, 4), lax.rem(self.y + dy, 4), lax.rem(self.x + dx, 4)
        core = lax.rem(self.core + dc, 2)
        return (y // 2) * 2 + core, z * 8 + lax.rem(y, 2) * 4 + x

    def partner(self, i):
        u, v, w, dc = lax.rem(i, 4), lax.rem(i // 4, 4), lax.rem(i // 16, 4), i // 64
        sign = 1 - 2 * self.core
        turn = lambda d: lax.rem(4 + sign * lax.rem(d, 4), 4)
        return self.at(turn(3 * u + 2 * v + w), turn(u + v), turn(u), dc)


def transfer(src, dst, sems, device):
    return pltpu.make_async_remote_copy(
        src_ref=src, dst_ref=dst, send_sem=sems.at[0], recv_sem=sems.at[1], device_id=device, device_id_type=MESH
    )


def scatter(place, src, dst, sems, own_sem):
    own = pltpu.make_async_copy(src.at[place.me], dst.at[place.me], own_sem)
    own.start()

    def send(i, carry):
        a, b = place.partner(i)
        transfer(src.at[a * 32 + b], dst.at[place.me], sems, (a, b)).start()
        return carry

    lax.fori_loop(1, DEVICES, send, 0)
    own.wait()


def all_chunks(place, src, dst, sems):
    others = pl.ds(0, DEVICES - 1)
    return transfer(src.at[others], dst.at[others], sems, place.at(0, 0, 1, 0))


def stage_modes(modes_ref, stage_ref, h):
    streams, spans, _ = modes_ref.shape
    half = streams // HALVES
    for k in range(half):
        stage_ref[pl.ds(k * WINDOW, spans), :] = modes_ref[h * half + k].astype(F32)


def synth_y(h, stage_ref, table, work_ref, flip_ref):
    cheb = stage_ref.shape[1]
    points = table.shape[0] if flip_ref is None else table.shape[0] // 2

    def columns(i, carry):
        lines = dot_nt(table, stage_ref[pl.ds(pl.multiple_of(i * BLOCK, BLOCK), BLOCK), :].astype(BF16))
        lane = pl.ds(pl.multiple_of(lax.rem(i, 2) * BLOCK, BLOCK), BLOCK)
        work_ref[2 * h + i // 2, 0:points, lane] = lines[0:points]
        if flip_ref is not None:
            flip_ref[h, :, pl.ds(pl.multiple_of(i * BLOCK, BLOCK), BLOCK)] = lines[points : points + cheb].astype(BF16)
        return carry

    lax.fori_loop(0, LANES // BLOCK, columns, 0)


def pack_chunks(work_ref, chunk_ref):
    rows = DEVICES * PLANES

    def pack(i, carry):
        lane = pl.ds(pl.multiple_of(lax.rem(i, 4) * TILE, TILE), TILE)
        low = work_ref[i // 4, 0:rows, lane].reshape(rows // 8, 8, TILE)
        high = work_ref[2 + i // 4, 0:rows, lane].reshape(rows // 8, 8, TILE)
        upper = rows_of(low.shape, 1) < 4
        even = jnp.where(upper, low, pltpu.roll(high, 4, 1))
        odd = jnp.where(upper, pltpu.roll(low, 4, 1), high)
        both = jnp.stack([even, odd], axis=1).reshape(DEVICES, 8, TILE)
        chunk_ref[:, :, pl.ds(pl.multiple_of(i * TILE, TILE), TILE)] = both.astype(BF16)
        return carry

    lax.fori_loop(0, LANES // TILE, pack, 0)


def unpack_rows(chunk_ref, h, at):
    chunk = chunk_ref[:, :, at].astype(F32)
    width = chunk.shape[2]
    pairs = chunk.reshape(DEVICES // 2, 2, 8, width)
    even, odd = pairs[:, 0], pairs[:, 1]
    upper = rows_of(even.shape, 1) < 4
    if h == 0:
        rows = jnp.where(upper, even, pltpu.roll(odd, 4, 1))
    else:
        rows = jnp.where(upper, pltpu.roll(even, 4, 1), odd)
    return rows.reshape(DEVICES * PLANES, width).astype(BF16)


def window_place(k):
    off = k * WINDOW
    first, shift = off // TILE, lax.rem(off, TILE)
    at = pl.ds(pl.multiple_of(first * TILE, TILE), TILE)
    after = pl.ds(pl.multiple_of((first + 1) * TILE, TILE), TILE)
    return shift, at, after


def synth_z(chunk_ref, table_ref, plane_ref, stage_ref, planes):
    group = DEVICES // 4
    rows = group * 8
    part = rows // PLANES

    def window(k, carry):
        shift, at, after = window_place(k)
        parts = []
        for a in range(4):
            own = pl.ds(a * group, group)
            left = chunk_ref[own, :, at].astype(F32).reshape(rows, TILE)
            right = chunk_ref[own, :, after].astype(F32).reshape(rows, TILE)
            mixed = jnp.where(rows_of(left.shape, 1) >= shift, left, right)
            parts.append(pltpu.roll(mixed, lax.rem(TILE - shift, TILE), 1).astype(BF16))
        points = dot(jnp.concatenate(parts, axis=1), table_ref[...])
        for c in range(NZ // TILE):
            stage_ref[c] = points[:, c * TILE : (c + 1) * TILE]
            for p in range(planes):
                plane_ref[p, pl.ds(pl.multiple_of(k * part, part), part), c * TILE : (c + 1) * TILE] = stage_ref[
                    c, pl.ds(p, part, stride=PLANES), :
                ].astype(BF16)
        return carry

    lax.fori_loop(0, 11, window, 0)


def analyse_z(stream_ref, table_ref, chunk_ref):
    group = DEVICES // 4

    def window(k, carry):
        shift, at, after = window_place(k)
        points = jnp.concatenate([stream_ref[k, c].astype(BF16) for c in range(NZ // TILE)], axis=1)
        lines = dot(points, table_ref[...])
        for a in range(4):
            own = pl.ds(a * group, group)
            moved = pltpu.roll(lines[:, a * TILE : (a + 1) * TILE], shift, 1).reshape(group, 8, TILE)
            keep = rows_of(moved.shape, 2) >= shift
            chunk_ref[own, :, at] = jnp.where(keep, moved, chunk_ref[own, :, at].astype(F32)).astype(BF16)
            chunk_ref[own, :, after] = moved.astype(BF16)
        return carry

    lax.fori_loop(0, 11, window, 0)


def keep_lines(stream_ref, lines, p, c):
    part = lines.shape[0] // 11
    for k in range(11):
        for t in range(BLOCK // TILE):
            stream_ref[k, c * (BLOCK // TILE) + t, pl.ds(p, part, stride=PLANES), :] = lines[
                k * part : (k + 1) * part, t * TILE : (t + 1) * TILE
            ]


def column_loop(body):
    def step(c, carry):
        body(c, pl.ds(pl.multiple_of(c * BLOCK, BLOCK), BLOCK))
        return carry

    lax.fori_loop(0, NZ // BLOCK, step, 0)


def gather_last(place, last_ref, sems):
    me, b = place.me, place.b
    own = pl.ds(me, 1)
    four, eight, all_x = pl.ds(place.a * 32 + (b // 4) * 4, 4), pl.ds(place.a * 32 + (b // 8) * 8, 8), pl.ds(place.a * 32, 32)
    other = lax.rem(place.a + 2, 4), b
    pair = place.at(0, 0, 0, 1)
    lower = pl.ds(place.core * 32, 32)
    upper = pl.ds(place.core * 32 + 64, 32)
    beside = place.a, (b // 8) * 8 + lax.rem(b // 4 + 1, 2) * 4 + place.x
    return [
        ([(own, place.at(0, 0, d, 0)) for d in (1, 2, 3)], 3),
        ([(four, beside)], 4),
        ([(eight, place.at(d, 0, 0, 0)) for d in (1, 2, 3)], 24),
        ([(all_x, other)], 32),
        ([(lower, pair), (upper, pair)], 64),
    ]


def kernel(
    phi_hbm, vel_hbm, both_hbm, synth_z_hbm, synth_x_hbm, analy_x_hbm, analy_z_hbm, analy_y_hbm, deriv_hbm, dual_hbm, basis_hbm,
    basis_t_hbm, own_x_ref, squares_ref, rates_ref, edge_ref, out_ref,
    modes_ref, both_ref, synth_z_ref, synth_x_ref, analy_x_ref, analy_z_ref, analy_y_ref, deriv_ref, dual_ref, basis_ref,
    basis_t_ref, stage_ref, work_ref, flip_ref, plane_ref, points_ref, stream_ref, slab_ref, last_ref, small_ref, extra_ref,
    phi_send, vel_send, phi_recv, vel_recv, cube_recv, flux_recv,
    table_sems, modes_sem, own_sem, phi_sems, vel_sems, cube_sems, flux_sems, last_sems,
):
    place = Place()
    cheb = dual_ref.shape[0]
    streams, spans, _ = out_ref.shape
    half = streams // HALVES

    modes_copy = pltpu.make_async_copy(phi_hbm, modes_ref, modes_sem)
    modes_copy.start()
    moves = {}
    pairs = dict(
        both=(both_hbm, both_ref), synth_z=(synth_z_hbm, synth_z_ref), synth_x=(synth_x_hbm, synth_x_ref),
        analy_x=(analy_x_hbm, analy_x_ref), analy_z=(analy_z_hbm, analy_z_ref), analy_y=(analy_y_hbm, analy_y_ref),
        deriv=(deriv_hbm, deriv_ref), dual=(dual_hbm, dual_ref), basis=(basis_hbm, basis_ref), basis_t=(basis_t_hbm, basis_t_ref),
    )
    for i, (name, (src, dst)) in enumerate(pairs.items()):
        moves[name] = pltpu.make_async_copy(src, dst, table_sems.at[i])
        moves[name].start()

    barrier = pltpu.get_barrier_semaphore()

    def greet(i, carry):
        pl.semaphore_signal(barrier, inc=1, device_id=place.partner(i), device_id_type=MESH)
        return carry

    lax.fori_loop(1, DEVICES, greet, 0)

    stage_ref[...] = jnp.zeros_like(stage_ref)
    modes_copy.wait()
    stage_modes(modes_ref, stage_ref, 0)
    moves["both"].wait()
    synth_y(0, stage_ref, both_ref[...], work_ref, flip_ref)
    stage_modes(modes_ref, stage_ref, 1)
    vel_copy = pltpu.make_async_copy(vel_hbm, modes_ref, modes_sem)
    vel_copy.start()
    synth_y(1, stage_ref, both_ref[...], work_ref, flip_ref)
    pack_chunks(work_ref, phi_send)
    pl.semaphore_wait(barrier, DEVICES - 1)
    scatter(place, phi_send, phi_recv, phi_sems, own_sem)
    for h in range(HALVES):
        for t in range(2):
            slab_ref[pl.ds(h * 4 + t * 2, 1), :] = work_ref[2 * h + t, pl.ds(cheb - 1, 1), :]

    vel_copy.wait()
    points_rows = both_ref.shape[0] // 2
    for h in range(HALVES):
        stage_modes(modes_ref, stage_ref, h)
        synth_y(h, stage_ref, both_ref[0:points_rows, :], work_ref, None)
    pack_chunks(work_ref, vel_send)
    for h in range(HALVES):
        for t in range(2):
            slab_ref[pl.ds(h * 4 + t * 2 + 1, 1), :] = work_ref[2 * h + t, pl.ds(cheb - 1, 1), :]
    last_ref[pl.ds(place.me, 1)] = slab_ref[...].astype(BF16).reshape(1, 8, WIDE)
    stages = gather_last(place, last_ref, last_sems)

    def gather_step(i):
        copies, total = stages[i]
        for rows, device in copies:
            transfer(last_ref.at[rows], last_ref.at[rows], last_sems.at[i], device).start()

    def gather_wait(i):
        copies, total = stages[i]
        block = pl.ds(0, total)
        done = transfer(last_ref.at[block], last_ref.at[block], last_sems.at[i], copies[0][1])
        done.wait_send()
        done.wait_recv()

    gather_step(0)
    scatter(place, vel_send, vel_recv, vel_sems, own_sem)
    for i in range(1, len(stages)):
        gather_wait(i - 1)
        gather_step(i)

    moves["synth_z"].wait()
    moves["synth_x"].wait()
    all_chunks(place, phi_send, phi_recv, phi_sems).wait_recv()
    synth_z(phi_recv, synth_z_ref, plane_ref, points_ref, PLANES)
    for p in range(PLANES):

        def phi_columns(c, at, p=p):
            work_ref[p, :, at] = dot(synth_x_ref[...], plane_ref[p, :, at])

        column_loop(phi_columns)

    all_chunks(place, vel_send, vel_recv, vel_sems).wait_recv()
    synth_z(vel_recv, synth_z_ref, plane_ref, points_ref, PLANES)
    moves["analy_x"].wait()
    moves["analy_z"].wait()
    for p in range(PLANES):

        def cube_columns(c, at, p=p):
            vel = dot(synth_x_ref[...], plane_ref[p, :, at])
            phi = work_ref[p, :, at]
            work_ref[p, :, at] = vel * phi
            keep_lines(stream_ref, dot(analy_x_ref[...], (phi * phi * phi).astype(BF16)), p, c)

        column_loop(cube_columns)

    all_chunks(place, phi_send, phi_recv, phi_sems).wait_send()
    phi_send[...] = jnp.zeros_like(phi_send)
    analyse_z(stream_ref, analy_z_ref, phi_send)
    scatter(place, phi_send, cube_recv, cube_sems, own_sem)
    for p in range(PLANES):

        def flux_columns(c, at, p=p):
            keep_lines(stream_ref, dot(analy_x_ref[...], work_ref[p, :, at].astype(BF16)), p, c)

        column_loop(flux_columns)

    all_chunks(place, vel_send, vel_recv, vel_sems).wait_send()
    vel_send[...] = jnp.zeros_like(vel_send)
    analyse_z(stream_ref, analy_z_ref, vel_send)
    scatter(place, vel_send, flux_recv, flux_sems, own_sem)

    gather_wait(len(stages) - 1)

    def spread(i, carry):
        some = pl.ds(pl.multiple_of(i * 16, 16), 16)
        chunk = last_ref[some]
        phi_recv[some, :, 0:WIDE] = chunk
        phi_recv[some, :, WIDE:LANES] = pltpu.roll(chunk.astype(F32), 6, 1).astype(BF16)
        return carry

    lax.fori_loop(0, DEVICES // 16, spread, 0)
    synth_z(phi_recv, synth_z_ref, plane_ref, points_ref, 2)

    def last_columns(c, at):
        phi = dot(synth_x_ref[...], plane_ref[0, :, at])
        vel = dot(synth_x_ref[...], plane_ref[1, :, at])
        small_ref[0, :, at] = dot(own_x_ref[...], (phi * phi * phi).astype(BF16)).astype(BF16)
        small_ref[1, :, at] = dot(own_x_ref[...], (vel * phi).astype(BF16)).astype(BF16)

    column_loop(last_columns)
    own_z = analy_z_ref[:, pl.ds(pl.multiple_of(place.a * TILE, TILE), TILE)]
    lane = rows_of((1, TILE), 1)
    for g in range(2):
        lines = dot(small_ref[g], own_z).astype(BF16).astype(F32)
        for h in range(HALVES):
            for k in range(half):
                first, shift = divmod(k * WINDOW, TILE)
                row = h * half + k
                moved = lines[row : row + 1]
                moved = pltpu.roll(moved, shift, 1) if shift else moved
                here = slice(first * TILE, (first + 1) * TILE)
                if shift:
                    moved_in = jnp.where(lane >= shift, moved, extra_ref[g, h, 0:1, here])
                else:
                    moved_in = moved
                extra_ref[g, h, 0:1, here] = moved_in
                extra_ref[g, h, 0:1, (first + 1) * TILE : (first + 2) * TILE] = moved

    for name in ("analy_y", "deriv", "dual", "basis", "basis_t"):
        moves[name].wait()
    eig = -rates_ref[...]
    all_chunks(place, phi_send, cube_recv, cube_sems).wait_recv()
    for h in range(HALVES):

        def lap_columns(i, carry, h=h):
            at = pl.ds(pl.multiple_of(i * WIDE, WIDE), WIDE)
            phi = flip_ref[h, :, at].astype(F32)
            cube = dot(analy_y_ref[...], unpack_rows(cube_recv, h, at)) + edge_ref[...] * extra_ref[0, h, 0:1, at]
            source = (cube - (1.0 + stabilizer) * phi).astype(BF16)
            scaled = ((eig - squares_ref[h, :, at]) * dot(dual_ref[...], source)).astype(BF16)
            work_ref[2 * h + i, 0:cheb, :] = dot(basis_ref[...], scaled)
            return carry

        lax.fori_loop(0, LANES // WIDE, lap_columns, 0)
    all_chunks(place, vel_send, flux_recv, flux_sems).wait_recv()
    for h in range(HALVES):
        for i in range(LANES // WIDE):
            start = i * WIDE
            at = pl.ds(start, WIDE)
            squares = squares_ref[h, :, at]
            phi = flip_ref[h, :, at].astype(F32)
            flux = dot(analy_y_ref[...], unpack_rows(flux_recv, h, at)) + edge_ref[...] * extra_ref[1, h, 0:1, at]
            slope = dot(deriv_ref[...], flux.astype(BF16))
            lap = work_ref[2 * h + i, 0:cheb, :]
            forcing = (
                (phi / time_step + mobility * lap - 8.0 / (cheb - 1) * slope) / (capillary * mobility)
            ).astype(BF16)
            first = (dot(dual_ref[...], forcing) / (eig - squares - screen_low)).astype(BF16)
            middle = dot(basis_ref[...], first).astype(BF16)
            second = (dot(dual_ref[...], middle) / (eig - squares - screen_high)).astype(BF16)
            result = dot_tn(second, basis_t_ref[...])
            for k in range(half):
                low, high = max(k * WINDOW, start), min(k * WINDOW + spans, start + WIDE)
                if low < high:
                    out_ref[h * half + k, low - k * WINDOW : high - k * WINDOW, :] = result[low - start : high - start]
    all_chunks(place, phi_send, cube_recv, cube_sems).wait_send()
    all_chunks(place, vel_send, flux_recv, flux_sems).wait_send()


def per_device(phi_hat, vel_hat, helm_basis, helm_dual, helm_rates):
    span_count = lax.axis_size("nz")
    stream_count = lax.axis_size("nx")
    span_local, stream_local, cheb = phi_hat.shape
    half = stream_local // HALVES
    a, b = lax.axis_index("nz"), lax.axis_index("nx")

    s_x, a_x, wave_x = fourier_tables(stream_local * stream_count, NX)
    s_z, a_z, wave_z = fourier_tables(span_local * span_count, NZ)
    s_y, a_y, d_y = chebyshev_tables(cheb)

    pad = -cheb % 16
    points = np.pad(s_y.T, ((0, pad), (0, 0)))
    both = np.concatenate([points, np.pad(np.eye(cheb, dtype=np.float32).astype(BF), ((0, pad), (0, 0)))])
    order = np.arange(stream_local * stream_count).reshape(stream_count, HALVES, half).transpose(2, 0, 1).reshape(-1)
    synth_x = np.ascontiguousarray(s_x.T[:, order])
    analy_x = np.ascontiguousarray(a_x.T[order])
    own_all = np.pad(a_x.T.reshape(stream_count, stream_local, NX), ((0, 0), (0, 32 - stream_local), (0, 0)))
    synth_z = np.pad(s_z.reshape(span_count, span_local, NZ), ((0, 0), (0, TILE - span_local), (0, 0))).reshape(-1, NZ)
    analy_z = np.pad(a_z.reshape(NZ, span_count, span_local), ((0, 0), (0, 0), (0, TILE - span_local))).reshape(NZ, -1)

    wave_s = lax.dynamic_slice_in_dim(jnp.asarray(wave_x), b * stream_local, stream_local)
    wave_p = lax.dynamic_slice_in_dim(jnp.asarray(wave_z), a * span_local, span_local)
    squares = wave_s[:, None] * wave_s[:, None] + wave_p[None, :] * wave_p[None, :]
    squares = jnp.pad(squares, ((0, 0), (0, WINDOW - span_local))).reshape(HALVES, 1, half * WINDOW)
    squares = jnp.pad(squares, ((0, 0), (0, 0), (0, LANES - half * WINDOW)))

    large = [
        jnp.transpose(phi_hat, (1, 0, 2)), jnp.transpose(vel_hat, (1, 0, 2)), jnp.asarray(both), jnp.asarray(synth_z),
        jnp.asarray(synth_x), jnp.asarray(analy_x), jnp.asarray(analy_z), jnp.asarray(np.ascontiguousarray(a_y[: cheb - 1].T)),
        jnp.asarray(np.ascontiguousarray(d_y.T)), helm_dual, helm_basis, helm_basis.T,
    ]
    small = [
        lax.dynamic_index_in_dim(jnp.asarray(own_all), b, 0, keepdims=False), squares, helm_rates[:, None],
        jnp.asarray(a_y[cheb - 1 :].T.astype(np.float32)),
    ]
    modes_x = stream_local * stream_count
    chunk = pltpu.VMEM((DEVICES, 8, LANES), BF16)
    sems = pltpu.SemaphoreType.DMA((2,))
    result = pl.pallas_call(
        kernel,
        out_shape=jax.ShapeDtypeStruct((stream_local, span_local, cheb), F32),
        in_specs=[pl.BlockSpec(memory_space=pl.ANY)] * len(large) + [pl.BlockSpec(memory_space=pltpu.VMEM)] * len(small),
        out_specs=pl.BlockSpec(memory_space=pltpu.VMEM),
        scratch_shapes=[pltpu.VMEM(large[0].shape, BF16)]
        + [pltpu.VMEM(table.shape, BF16) for table in large[2:]]
        + [
            pltpu.VMEM((LANES, cheb), F32),
            pltpu.VMEM((PLANES, NX, NZ), F32),
            pltpu.VMEM((HALVES, cheb, LANES), BF16),
            pltpu.VMEM((PLANES, modes_x, NZ), BF16),
            pltpu.VMEM((NZ // TILE, 256, TILE), F32),
            pltpu.VMEM((11, NZ // TILE, 256, TILE), F32),
            pltpu.VMEM((8, WIDE), F32),
            pltpu.VMEM((DEVICES, 8, WIDE), BF16),
            pltpu.VMEM((2, 32, NZ), BF16),
            pltpu.VMEM((2, HALVES, 8, LANES), F32),
        ]
        + [chunk] * 6
        + [
            pltpu.SemaphoreType.DMA((len(large) - 2,)), pltpu.SemaphoreType.DMA, pltpu.SemaphoreType.DMA,
            sems, sems, sems, sems, pltpu.SemaphoreType.DMA((5, 2)),
        ],
        compiler_params=pltpu.CompilerParams(collective_id=0, has_side_effects=True, vmem_limit_bytes=60 << 20),
    )(*large, *small)
    return jnp.transpose(result, (1, 0, 2))


def solution(mesh):
    placed = (P("nz", "nx", None), P("nz", "nx", None), P(), P(), P())
    return jax.shard_map(
        per_device, mesh=mesh, in_specs=placed, out_specs=P("nz", "nx", None), check_vma=False
    )
```

```python
import math

import jax
import jax.numpy as jnp
import ml_dtypes
import numpy as np
from jax import lax
from jax.experimental import pallas as pl
from jax.experimental.pallas import tpu as pltpu
from jax.sharding import PartitionSpec as P

NX = 1024
NZ = 512

mobility = 1.0
capillary = 0.2
screen_low = 4.0
screen_high = 20.0
time_step = 1.0 / (screen_low * screen_high * mobility * capillary)
stabilizer = capillary * (screen_low + screen_high)

PLANES = 4
HALVES = 2
WINDOW = 88
LANES = 1024
TILE = 128
BF = ml_dtypes.bfloat16
F32 = jnp.float32
BF16 = jnp.bfloat16


def fourier_tables(mode_count, point_count):
    half_count = mode_count // 2
    mode_index = np.arange(mode_count)
    wave_index = np.where(mode_index < half_count, mode_index, mode_index - half_count + 1)
    phase_steps = wave_index[:, None] * np.arange(point_count)[None, :] % point_count
    angles = phase_steps * (2.0 * math.pi / point_count)
    basis = np.where((mode_index < half_count)[:, None], np.cos(angles), np.sin(angles))
    factor = math.sqrt(2.0 / mode_count)
    weights = np.where(mode_index == 0, 1.0, 2.0) / (point_count * factor)
    return (
        (factor * basis).astype(np.float32).astype(BF),
        (basis.T * weights[None, :]).astype(np.float32).astype(BF),
    )


def chebyshev_tables(count):
    index = np.arange(count)
    phase_steps = index[:, None] * index[None, :] % (2 * (count - 1))
    cosines = np.cos(phase_steps * (math.pi / (count - 1)))
    factor = math.sqrt(2.0 / count)
    ends = np.where((index == 0) | (index == count - 1), 2.0, 1.0)
    analysis = cosines.T * (2.0 / ((count - 1) * factor)) / (ends[:, None] * ends[None, :])
    upper, lower = index[:, None], index[None, :]
    deriv = np.where((upper > lower) & ((upper + lower) % 2 == 1), 2.0 * upper / ends[None, :], 0.0)
    as_bf = lambda t: t.astype(np.float32).astype(BF)
    return as_bf(factor * cosines), as_bf(analysis), as_bf(deriv)


def dot(left, right):
    return jnp.dot(left, right, preferred_element_type=F32)


def dot_nt(left, right):
    return lax.dot_general(left, right, (((1,), (1,)), ((), ())), preferred_element_type=F32)


def dot_tn(left, right):
    return lax.dot_general(left, right, (((0,), (0,)), ((), ())), preferred_element_type=F32)


def rows_of(shape, axis):
    return lax.broadcasted_iota(jnp.int32, shape, axis)


MESH = pl.DeviceIdType.MESH
DEVICES = 128
BLOCK = 256
WIDE = 512


class Place:
    def __init__(self):
        self.a, self.b = lax.axis_index("nz"), lax.axis_index("nx")
        self.me = self.a * 32 + self.b
        self.core = self.a & 1
        self.beside = (self.a, self.b ^ 1)
        self.sign = 1 - 2 * self.core
        y = (self.a >> 1) * 2 + ((self.b >> 2) & 1)
        ys = [(y + self.sign * d) & 3 for d in range(4)]
        self.xs = [(self.b + self.sign * d) & 3 for d in range(4)]
        self.ys = [((d >> 1) * 2, (d & 1) * 4) for d in ys]
        self.z = self.b >> 3

    def each(self, visit):
        def some(j, carry):
            core = self.core ^ (j >> 2)
            z = self.z + self.sign * (j & 3)
            for v in range(4):
                for u in range(4):
                    y_hi, y_lo = self.ys[(u + v) & 3]
                    nz = y_hi + core
                    nx = ((z + self.sign * (3 * u + 2 * v)) & 3) * 8 + y_lo + self.xs[u]
                    if u or v:
                        visit(nz, nx)
                    else:
                        pl.when(j > 0)(lambda nz=nz, nx=nx: visit(nz, nx))
            return carry

        lax.fori_loop(0, 8, some, 0)


def transfer(src, dst, sems, device):
    return pltpu.make_async_remote_copy(
        src_ref=src, dst_ref=dst, send_sem=sems.at[0], recv_sem=sems.at[1], device_id=device, device_id_type=MESH
    )


def scatter(place, src, dst, sems, own_sem):
    own = pltpu.make_async_copy(src.at[place.me], dst.at[place.me], own_sem)
    own.start()

    def send(a, b):
        transfer(src.at[a * 32 + b], dst.at[place.me], sems, (a, b)).start()

    place.each(send)
    own.wait()


def all_chunks(place, src, dst, sems):
    others = pl.ds(0, DEVICES - 1)
    return transfer(src.at[others], dst.at[others], sems, place.beside)


def stage_modes(modes_ref, stage_ref, h):
    streams, spans, _ = modes_ref.shape
    half = streams // HALVES
    for k in range(half):
        stage_ref[pl.ds(k * WINDOW, spans), :] = modes_ref[h * half + k].astype(F32)


def synth_y(h, stage_ref, table_ref, work_ref):
    def columns(i, carry):
        lines = dot_nt(table_ref[...], stage_ref[pl.ds(pl.multiple_of(i * BLOCK, BLOCK), BLOCK), :].astype(BF16))
        lane = pl.ds(pl.multiple_of((i & 1) * BLOCK, BLOCK), BLOCK)
        work_ref[2 * h + (i >> 1), 0 : lines.shape[0], lane] = lines
        return carry

    lax.fori_loop(0, LANES // BLOCK, columns, 0)


def pack_chunks(work_ref, chunk_ref):
    rows = DEVICES * PLANES

    def pack(i, carry):
        lane = pl.ds(pl.multiple_of((i & 3) * TILE, TILE), TILE)
        low = work_ref[i >> 2, 0:rows, lane].reshape(rows // 8, 8, TILE)
        high = work_ref[2 + (i >> 2), 0:rows, lane].reshape(rows // 8, 8, TILE)
        upper = rows_of(low.shape, 1) < 4
        even = jnp.where(upper, low, pltpu.roll(high, 4, 1))
        odd = jnp.where(upper, pltpu.roll(low, 4, 1), high)
        both = jnp.stack([even, odd], axis=1).reshape(DEVICES, 8, TILE)
        chunk_ref[:, :, pl.ds(pl.multiple_of(i * TILE, TILE), TILE)] = both.astype(BF16)
        return carry

    lax.fori_loop(0, LANES // TILE, pack, 0)


def unpack_rows(chunk_ref, h, at):
    chunk = chunk_ref[:, :, at].astype(F32)
    width = chunk.shape[2]
    pairs = chunk.reshape(DEVICES // 2, 2, 8, width)
    even, odd = pairs[:, 0], pairs[:, 1]
    upper = rows_of(even.shape, 1) < 4
    if h == 0:
        rows = jnp.where(upper, even, pltpu.roll(odd, 4, 1))
    else:
        rows = jnp.where(upper, pltpu.roll(even, 4, 1), odd)
    return rows.reshape(DEVICES * PLANES, width).astype(BF16)


def window_place(k):
    off = k * WINDOW
    first, shift = off >> 7, off & (TILE - 1)
    at = pl.ds(pl.multiple_of(first * TILE, TILE), TILE)
    after = pl.ds(pl.multiple_of((first + 1) * TILE, TILE), TILE)
    return shift, at, after


def synth_z(chunk_ref, table_ref, plane_ref, stage_ref, planes):
    group = DEVICES // 4
    rows = group * 8
    part = rows // PLANES

    def window(k, carry):
        shift, at, after = window_place(k)
        parts = []
        for a in range(4):
            own = pl.ds(a * group, group)
            left = chunk_ref[own, :, at].astype(F32).reshape(rows, TILE)
            right = chunk_ref[own, :, after].astype(F32).reshape(rows, TILE)
            mixed = jnp.where(rows_of(left.shape, 1) >= shift, left, right)
            parts.append(pltpu.roll(mixed, (TILE - shift) & (TILE - 1), 1).astype(BF16))
        points = dot(jnp.concatenate(parts, axis=1), table_ref[...])
        for c in range(NZ // TILE):
            stage_ref[c] = points[:, c * TILE : (c + 1) * TILE]
            for p in range(planes):
                plane_ref[p, pl.ds(pl.multiple_of(k * part, part), part), c * TILE : (c + 1) * TILE] = stage_ref[
                    c, pl.ds(p, part, stride=PLANES), :
                ].astype(BF16)
        return carry

    lax.fori_loop(0, 11, window, 0)


def analyse_z(stream_ref, table_ref, chunk_ref):
    group = DEVICES // 4

    def window(k, carry):
        shift, at, after = window_place(k)
        points = jnp.concatenate([stream_ref[k, c].astype(BF16) for c in range(NZ // TILE)], axis=1)
        lines = dot(points, table_ref[...])
        for a in range(4):
            own = pl.ds(a * group, group)
            moved = pltpu.roll(lines[:, a * TILE : (a + 1) * TILE], shift, 1).reshape(group, 8, TILE)
            keep = rows_of(moved.shape, 2) >= shift
            chunk_ref[own, :, at] = jnp.where(keep, moved, chunk_ref[own, :, at].astype(F32)).astype(BF16)
            chunk_ref[own, :, after] = moved.astype(BF16)
        return carry

    lax.fori_loop(0, 11, window, 0)


def keep_lines(stream_ref, lines, p, c):
    part = lines.shape[0] // 11
    for k in range(11):
        for t in range(BLOCK // TILE):
            stream_ref[k, c * (BLOCK // TILE) + t, pl.ds(p, part, stride=PLANES), :] = lines[
                k * part : (k + 1) * part, t * TILE : (t + 1) * TILE
            ]


def column_loop(body):
    def step(c, carry):
        body(c, pl.ds(pl.multiple_of(c * BLOCK, BLOCK), BLOCK))
        return carry

    lax.fori_loop(0, NZ // BLOCK, step, 0)


SPARE = 72
LAST = slice(LANES - TILE, LANES)


def last_out(place, work_ref, table_ref, rows_ref):
    lane = rows_of((1, TILE), 1)
    points = DEVICES * PLANES
    table = table_ref[:, pl.ds(pl.multiple_of(place.a * TILE, TILE), TILE)]
    for h in range(HALVES):
        for k in range(11):
            first, shift = divmod(k * WINDOW, TILE)
            tile = lambda t: work_ref[2 * h + t // 4, points : points + 1, (t % 4) * TILE : (t % 4 + 1) * TILE]
            row = tile(first)
            if shift:
                row = pltpu.roll(jnp.where(lane >= shift, row, tile(first + 1)), TILE - shift, 1)
            rows_ref[SPARE + k : SPARE + k + 1, :] = row
        work_ref[2 * h + 1, 0:points, WIDE - TILE : WIDE] += dot_nt(table, rows_ref[...].astype(BF16))


def last_in(chunk_ref, points_ref, last_ref):
    group = DEVICES // 4
    total = chunk_ref[0:group, :, LAST].astype(F32)
    for a in range(1, 4):
        total = total + chunk_ref[a * group : (a + 1) * group, :, LAST].astype(F32)
    points_ref[0] = total.reshape(group * 8, TILE)
    part = group * HALVES
    lines = [points_ref[0, pl.ds(p, part, stride=PLANES), :] for p in range(PLANES)]
    lane = rows_of((part, TILE), 1)
    for k in range(11):
        rows = jnp.zeros((part, TILE), F32)
        for p in range(PLANES):
            rows = jnp.where(lane == p, lines[p][:, SPARE + k : SPARE + k + 1], rows)
        last_ref[k * part : (k + 1) * part, :] = rows.astype(BF16)


def last_back(lines, points_ref):
    part = lines.shape[0] // 11
    lane = rows_of((part, TILE), 1)
    for p in range(PLANES):
        rows = jnp.zeros((part, TILE), F32)
        for k in range(11):
            rows = jnp.where(lane == SPARE + k, lines[k * part : (k + 1) * part, p : p + 1], rows)
        points_ref[1, pl.ds(p, part, stride=PLANES), :] = rows


def last_fill(points_ref, chunk_ref):
    group = DEVICES // 4
    rows = points_ref[1].reshape(group, 8, TILE)
    keep = rows_of(rows.shape, 2) < SPARE
    for a in range(4):
        own = slice(a * group, (a + 1) * group)
        chunk_ref[own, :, LAST] = jnp.where(keep, chunk_ref[own, :, LAST].astype(F32), rows).astype(BF16)


def last_edge(place, chunk_ref, table_ref, edge_ref):
    table = table_ref[:, pl.ds(pl.multiple_of(place.a * TILE, TILE), TILE)]
    lane = rows_of((1, TILE), 1)
    for h in range(HALVES):
        lines = dot_tn(unpack_rows(chunk_ref, h, LAST), table).astype(BF16).astype(F32)
        for k in range(11):
            first, shift = divmod(k * WINDOW, TILE)
            moved = lines[SPARE + k : SPARE + k + 1]
            here, after = slice(first * TILE, (first + 1) * TILE), slice((first + 1) * TILE, (first + 2) * TILE)
            if shift:
                moved = pltpu.roll(moved, shift, 1)
                edge_ref[h, 0:1, here] = jnp.where(lane >= shift, moved, edge_ref[h, 0:1, here])
            else:
                edge_ref[h, 0:1, here] = moved
            edge_ref[h, 0:1, after] = moved


def wave_squares(place, half_span, half_stream, span_local, stream_local, h, start):
    lane = start + rows_of((1, WIDE), 1)
    k, j = lane // WINDOW, lane % WINDOW

    def squared(mode, count):
        wave = 2.0 * jnp.where(mode < count, mode, mode - count + 1).astype(F32) / count
        return wave * wave

    stream = squared(place.b * stream_local + h * (stream_local // HALVES) + k, half_stream)
    return squared(place.a * span_local + j, half_span) + stream


def kernel(
    phi_hbm, vel_hbm, points_hbm, synth_zt_hbm, synth_z_hbm, synth_x_hbm, analy_x_hbm, analy_z_hbm, analy_y_hbm, slope_hbm,
    dual_hbm, basis_hbm, rates_ref, out_ref,
    modes_ref, table_y_ref, synth_zt_ref, synth_z_ref, synth_x_ref, analy_x_ref, analy_z_ref, analy_y_ref, slope_ref,
    dual_ref, basis_ref, stage_ref, work_ref, solve_ref, plane_ref, points_ref, stream_ref, rows_ref, last_ref, last_phi_ref,
    edge_ref, eig_ref, cube_table, flux_table, both_table, ends_ref,
    phi_send, vel_send, phi_recv, vel_recv, cube_recv, flux_recv,
    table_sems, modes_sem, own_sem, phi_sems, vel_sems, cube_sems, flux_sems,
):
    place = Place()
    cheb = dual_ref.shape[0]
    streams, spans, _ = modes_ref.shape
    rows = cheb - 1

    modes_copy = pltpu.make_async_copy(phi_hbm, modes_ref, modes_sem)
    modes_copy.start()
    moves = {}
    pairs = dict(
        points=(points_hbm, table_y_ref), synth_zt=(synth_zt_hbm, synth_zt_ref), dual=(dual_hbm, dual_ref),
        analy_y=(analy_y_hbm, analy_y_ref), slope=(slope_hbm, slope_ref), basis=(basis_hbm, basis_ref),
        synth_z=(synth_z_hbm, synth_z_ref), synth_x=(synth_x_hbm, synth_x_ref), analy_x=(analy_x_hbm, analy_x_ref),
        analy_z=(analy_z_hbm, analy_z_ref),
    )
    for i, (name, (src, dst)) in enumerate(pairs.items()):
        moves[name] = pltpu.make_async_copy(src, dst, table_sems.at[i])
        moves[name].start()

    barrier = pltpu.get_barrier_semaphore()

    def greet(a, b):
        pl.semaphore_signal(barrier, inc=1, device_id=(a, b), device_id_type=MESH)

    place.each(greet)

    stage_ref[...] = jnp.zeros_like(stage_ref)
    rows_ref[...] = jnp.zeros_like(rows_ref)
    modes_copy.wait()
    stage_modes(modes_ref, stage_ref, 0)
    moves["points"].wait()
    synth_y(0, stage_ref, table_y_ref, work_ref)
    stage_modes(modes_ref, stage_ref, 1)
    synth_y(1, stage_ref, table_y_ref, work_ref)
    moves["synth_zt"].wait()
    last_out(place, work_ref, synth_zt_ref, rows_ref)
    pack_chunks(work_ref, phi_send)
    pl.semaphore_wait(barrier, DEVICES - 1)
    scatter(place, phi_send, phi_recv, phi_sems, own_sem)

    moves["dual"].wait()
    for h in (1, 0):
        if h == 0:
            stage_modes(modes_ref, stage_ref, 0)
            vel_copy = pltpu.make_async_copy(vel_hbm, modes_ref, modes_sem)
            vel_copy.start()

        def dual_columns(i, carry, h=h):
            at = pl.ds(pl.multiple_of(i * BLOCK, BLOCK), BLOCK)
            solve_ref[h, :, at] = dot_nt(dual_ref[...], stage_ref[at, :].astype(BF16))
            return carry

        lax.fori_loop(0, LANES // BLOCK, dual_columns, 0)

    vel_copy.wait()
    for h in range(HALVES):
        stage_modes(modes_ref, stage_ref, h)
        synth_y(h, stage_ref, table_y_ref, work_ref)
    last_out(place, work_ref, synth_zt_ref, rows_ref)
    pack_chunks(work_ref, vel_send)
    scatter(place, vel_send, vel_recv, vel_sems, own_sem)

    for name in ("analy_y", "slope", "basis"):
        moves[name].wait()
    for n, (left, product) in enumerate(((analy_y_ref, cube_table), (slope_ref, flux_table))):
        full = dot(dual_ref[...], left[...])
        product[...] = full[:, 0:rows].astype(BF16)
        ends_ref[n] = jnp.broadcast_to(full[:, rows:cheb], (cheb, TILE))
    both_table[...] = dot(dual_ref[...], basis_ref[...]).astype(BF16)
    eig_ref[0:rows, :] = -jnp.transpose(jnp.broadcast_to(rates_ref[:, 0:rows], (TILE, rows)))
    eig_ref[rows:cheb, :] = -jnp.broadcast_to(rates_ref[:, rows:cheb], (1, TILE))

    for name in ("synth_z", "synth_x", "analy_x", "analy_z"):
        moves[name].wait()
    all_chunks(place, phi_send, phi_recv, phi_sems).wait_recv()
    synth_z(phi_recv, synth_z_ref, plane_ref, points_ref, PLANES)
    for p in range(PLANES):

        def cube_columns(c, at, p=p):
            phi = dot(synth_x_ref[...], plane_ref[p, :, at])
            work_ref[p, :, at] = phi
            keep_lines(stream_ref, dot(analy_x_ref[...], (phi * phi * phi).astype(BF16)), p, c)

        column_loop(cube_columns)

    last_in(phi_recv, points_ref, last_ref)
    phi = dot(synth_x_ref[...], last_ref[...])
    last_phi_ref[...] = phi
    last_back(dot(analy_x_ref[...], (phi * phi * phi).astype(BF16)), points_ref)
    all_chunks(place, phi_send, phi_recv, phi_sems).wait_send()
    analyse_z(stream_ref, analy_z_ref, phi_send)
    last_fill(points_ref, phi_send)
    scatter(place, phi_send, cube_recv, cube_sems, own_sem)

    all_chunks(place, vel_send, vel_recv, vel_sems).wait_recv()
    synth_z(vel_recv, synth_z_ref, plane_ref, points_ref, PLANES)
    for p in range(PLANES):

        def flux_columns(c, at, p=p):
            flux = dot(synth_x_ref[...], plane_ref[p, :, at]) * work_ref[p, :, at]
            keep_lines(stream_ref, dot(analy_x_ref[...], flux.astype(BF16)), p, c)

        column_loop(flux_columns)

    last_in(vel_recv, points_ref, last_ref)
    flux = dot(synth_x_ref[...], last_ref[...]) * last_phi_ref[...]
    last_back(dot(analy_x_ref[...], flux.astype(BF16)), points_ref)
    all_chunks(place, vel_send, vel_recv, vel_sems).wait_send()
    analyse_z(stream_ref, analy_z_ref, vel_send)
    last_fill(points_ref, vel_send)
    scatter(place, vel_send, flux_recv, flux_sems, own_sem)

    def squares_at(h, start):
        return wave_squares(place, spans * 2, streams * 16, spans, streams, h, start)

    eig = eig_ref[:, 0:1]
    all_chunks(place, phi_send, cube_recv, cube_sems).wait_recv()
    last_edge(place, cube_recv, analy_z_ref, edge_ref)
    for h in range(HALVES):

        def lap_columns(i, carry, h=h):
            at = pl.ds(pl.multiple_of(i * WIDE, WIDE), WIDE)
            phi = solve_ref[h, :, at]
            cube = dot(cube_table[...], unpack_rows(cube_recv, h, at)) + ends_ref[0, :, 0:1] * edge_ref[h, 0:1, at]
            scaled = (eig - squares_at(h, i * WIDE)) * (cube - (1.0 + stabilizer) * phi)
            lap = dot(both_table[...], scaled.astype(BF16))
            solve_ref[h, :, at] = (phi / time_step + mobility * lap) / (capillary * mobility)
            return carry

        lax.fori_loop(0, LANES // WIDE, lap_columns, 0)
    all_chunks(place, vel_send, flux_recv, flux_sems).wait_recv()
    last_edge(place, flux_recv, analy_z_ref, edge_ref)
    for h in range(HALVES):

        def solve_columns(i, carry, h=h):
            at = pl.ds(pl.multiple_of(i * WIDE, WIDE), WIDE)
            shifted = eig - squares_at(h, i * WIDE)
            slope = dot(flux_table[...], unpack_rows(flux_recv, h, at)) + ends_ref[1, :, 0:1] * edge_ref[h, 0:1, at]
            forcing = solve_ref[h, :, at] - 8.0 / (cheb - 1) / (capillary * mobility) * slope
            first = (forcing / (shifted - screen_low)).astype(BF16)
            out_ref[h, :, at] = (dot(both_table[...], first) / (shifted - screen_high)).astype(BF16)
            return carry

        lax.fori_loop(0, LANES // WIDE, solve_columns, 0)
    all_chunks(place, phi_send, cube_recv, cube_sems).wait_send()
    all_chunks(place, vel_send, flux_recv, flux_sems).wait_send()


def finish_kernel(second_ref, basis_ref, out_ref):
    half, spans, _ = out_ref.shape
    for start in range(0, LANES, BLOCK):
        result = lax.dot_general(
            second_ref[0, :, start : start + BLOCK], basis_ref[...], (((0,), (1,)), ((), ())), preferred_element_type=F32
        )
        for k in range(half):
            low, high = max(k * WINDOW, start), min(k * WINDOW + spans, start + BLOCK)
            if low < high:
                out_ref[k, low - k * WINDOW : high - k * WINDOW, :] = result[low - start : high - start]


def per_device(phi_hat, vel_hat, helm_basis, helm_dual, helm_rates):
    span_count = lax.axis_size("nz")
    stream_count = lax.axis_size("nx")
    span_local, stream_local, cheb = phi_hat.shape
    half = stream_local // HALVES
    s_x, a_x = fourier_tables(stream_local * stream_count, NX)
    s_z, a_z = fourier_tables(span_local * span_count, NZ)
    s_y, a_y, d_y = chebyshev_tables(cheb)

    points = np.pad(s_y.T, ((0, -cheb % 8), (0, 0)))
    slope = (d_y.astype(np.float64).T @ a_y.astype(np.float64).T).astype(np.float32).astype(BF)
    order = np.arange(stream_local * stream_count).reshape(stream_count, HALVES, half).transpose(2, 0, 1).reshape(-1)
    synth_x = np.ascontiguousarray(s_x.T[:, order])
    analy_x = np.ascontiguousarray(a_x.T[order])
    synth_z = np.pad(s_z.reshape(span_count, span_local, NZ), ((0, 0), (0, TILE - span_local), (0, 0))).reshape(-1, NZ)
    analy_z = np.pad(a_z.reshape(NZ, span_count, span_local), ((0, 0), (0, 0), (0, TILE - span_local))).reshape(NZ, -1)

    large = [jnp.transpose(phi_hat, (1, 0, 2)), jnp.transpose(vel_hat, (1, 0, 2))]
    tables = (points, np.ascontiguousarray(synth_z.T), synth_z, synth_x, analy_x, analy_z, np.ascontiguousarray(a_y.T), slope)
    large += [jnp.asarray(table) for table in tables] + [helm_dual, helm_basis]
    modes_x = stream_local * stream_count
    chunk = pltpu.VMEM((DEVICES, 8, LANES), BF16)
    sems = pltpu.SemaphoreType.DMA((2,))
    second = pl.pallas_call(
        kernel,
        out_shape=jax.ShapeDtypeStruct((HALVES, cheb, LANES), BF16),
        in_specs=[pl.BlockSpec(memory_space=pl.ANY)] * len(large) + [pl.BlockSpec(memory_space=pltpu.VMEM)],
        out_specs=pl.BlockSpec(memory_space=pltpu.VMEM),
        scratch_shapes=[pltpu.VMEM(large[0].shape, BF16)]
        + [pltpu.VMEM(table.shape, BF16) for table in large[2:]]
        + [
            pltpu.VMEM((LANES, cheb), F32),
            pltpu.VMEM((PLANES, NX, NZ), F32),
            pltpu.VMEM((HALVES, cheb, LANES), F32),
            pltpu.VMEM((PLANES, modes_x, NZ), BF16),
            pltpu.VMEM((NZ // TILE, 256, TILE), F32),
            pltpu.VMEM((11, NZ // TILE, 256, TILE), F32),
            pltpu.VMEM((TILE, TILE), F32),
            pltpu.VMEM((modes_x, TILE), BF16),
            pltpu.VMEM((NX, TILE), F32),
            pltpu.VMEM((HALVES, 8, LANES), F32),
            pltpu.VMEM((cheb, TILE), F32),
            pltpu.VMEM((cheb, cheb - 1), BF16),
            pltpu.VMEM((cheb, cheb - 1), BF16),
            pltpu.VMEM((cheb, cheb), BF16),
            pltpu.VMEM((2, cheb, TILE), F32),
        ]
        + [chunk] * 6
        + [
            pltpu.SemaphoreType.DMA((len(large) - 2,)), pltpu.SemaphoreType.DMA, pltpu.SemaphoreType.DMA,
            sems, sems, sems, sems,
        ],
        compiler_params=pltpu.CompilerParams(collective_id=0, has_side_effects=True, vmem_limit_bytes=60 << 20),
    )(*large, helm_rates.reshape(1, cheb))
    result = pl.pallas_call(
        finish_kernel,
        out_shape=jax.ShapeDtypeStruct((stream_local, span_local, cheb), F32),
        grid=(HALVES,),
        in_specs=[pl.BlockSpec((1, cheb, LANES), lambda h: (h, 0, 0)), pl.BlockSpec((cheb, cheb), lambda h: (0, 0))],
        out_specs=pl.BlockSpec((half, span_local, cheb), lambda h: (h, 0, 0)),
        compiler_params=pltpu.CompilerParams(vmem_limit_bytes=40 << 20),
    )(second, helm_basis)
    return jnp.transpose(result, (1, 0, 2))


def solution(mesh):
    placed = (P("nz", "nx", None), P("nz", "nx", None), P(), P(), P())
    return jax.shard_map(
        per_device, mesh=mesh, in_specs=placed, out_specs=P("nz", "nx", None), check_vma=False
    )
```

```python
import math

import jax
import jax.numpy as jnp
import ml_dtypes
import numpy as np
from jax import lax
from jax.experimental import pallas as pl
from jax.experimental.pallas import tpu as pltpu
from jax.sharding import PartitionSpec as P

NX = 1024
NZ = 512

mobility = 1.0
capillary = 0.2
screen_low = 4.0
screen_high = 20.0
time_step = 1.0 / (screen_low * screen_high * mobility * capillary)
stabilizer = capillary * (screen_low + screen_high)

PLANES = 4
HALVES = 2
WINDOW = 88
LANES = 1024
TILE = 128
BF = ml_dtypes.bfloat16
F32 = jnp.float32
BF16 = jnp.bfloat16


def fourier_tables(mode_count, point_count):
    half_count = mode_count // 2
    mode_index = np.arange(mode_count)
    wave_index = np.where(mode_index < half_count, mode_index, mode_index - half_count + 1)
    phase_steps = wave_index[:, None] * np.arange(point_count)[None, :] % point_count
    angles = phase_steps * (2.0 * math.pi / point_count)
    basis = np.where((mode_index < half_count)[:, None], np.cos(angles), np.sin(angles))
    factor = math.sqrt(2.0 / mode_count)
    weights = np.where(mode_index == 0, 1.0, 2.0) / (point_count * factor)
    return (
        (factor * basis).astype(np.float32).astype(BF),
        (basis.T * weights[None, :]).astype(np.float32).astype(BF),
    )


def chebyshev_tables(count):
    index = np.arange(count)
    phase_steps = index[:, None] * index[None, :] % (2 * (count - 1))
    cosines = np.cos(phase_steps * (math.pi / (count - 1)))
    factor = math.sqrt(2.0 / count)
    ends = np.where((index == 0) | (index == count - 1), 2.0, 1.0)
    analysis = cosines.T * (2.0 / ((count - 1) * factor)) / (ends[:, None] * ends[None, :])
    upper, lower = index[:, None], index[None, :]
    deriv = np.where((upper > lower) & ((upper + lower) % 2 == 1), 2.0 * upper / ends[None, :], 0.0)
    as_bf = lambda t: t.astype(np.float32).astype(BF)
    return as_bf(factor * cosines), as_bf(analysis), as_bf(deriv)


def dot(left, right):
    return jnp.dot(left, right, preferred_element_type=F32)


def dot_nt(left, right):
    return lax.dot_general(left, right, (((1,), (1,)), ((), ())), preferred_element_type=F32)


def dot_tn(left, right):
    return lax.dot_general(left, right, (((0,), (0,)), ((), ())), preferred_element_type=F32)


def rows_of(shape, axis):
    return lax.broadcasted_iota(jnp.int32, shape, axis)


MESH = pl.DeviceIdType.MESH
DEVICES = 128
BLOCK = 256
WIDE = 512
BASE = LANES - 11 * WINDOW


class Place:
    def __init__(self):
        self.a, self.b = lax.axis_index("nz"), lax.axis_index("nx")
        self.me = self.a * 32 + self.b
        self.core = self.a & 1
        self.beside = (self.a, self.b ^ 1)
        self.sign = 1 - 2 * self.core
        y = (self.a >> 1) * 2 + ((self.b >> 2) & 1)
        ys = [(y + self.sign * d) & 3 for d in range(4)]
        self.xs = [(self.b + self.sign * d) & 3 for d in range(4)]
        self.ys = [((d >> 1) * 2, (d & 1) * 4) for d in ys]
        self.z = self.b >> 3

    def each(self, visit):
        def some(j, carry):
            core = self.core ^ (j >> 2)
            z = self.z + self.sign * (j & 3)
            for v in range(4):
                for u in range(4):
                    y_hi, y_lo = self.ys[(u + v) & 3]
                    nz = y_hi + core
                    nx = ((z + self.sign * (3 * u + 2 * v)) & 3) * 8 + y_lo + self.xs[u]
                    if u or v:
                        visit(nz, nx)
                    else:
                        pl.when(j > 0)(lambda nz=nz, nx=nx: visit(nz, nx))
            return carry

        lax.fori_loop(0, 8, some, 0)


def transfer(src, dst, sems, device):
    return pltpu.make_async_remote_copy(
        src_ref=src, dst_ref=dst, send_sem=sems.at[0], recv_sem=sems.at[1], device_id=device, device_id_type=MESH
    )


def lanes_of(g):
    return slice(g * WIDE, (g + 1) * WIDE)


def scatter(place, src, dst, sems, own_sem, g):
    own = pltpu.make_async_copy(src.at[place.me, :, lanes_of(g)], dst.at[place.me, :, lanes_of(g)], own_sem)
    own.start()

    def send(a, b):
        transfer(src.at[a * 32 + b, :, lanes_of(g)], dst.at[place.me, :, lanes_of(g)], sems.at[g], (a, b)).start()

    place.each(send)
    own.wait()


def all_chunks(place, src, dst, sems, g):
    others = pl.ds(0, DEVICES - 1)
    return transfer(src.at[others, :, lanes_of(g)], dst.at[others, :, lanes_of(g)], sems.at[g], place.beside)


def stage_modes(modes_ref, stage_ref, g, base):
    streams, spans, _ = modes_ref.shape
    half = streams // HALVES
    for h in range(HALVES):
        for k in range(half):
            off = base + k * WINDOW
            low, high = max(off, g * WIDE), min(off + spans, (g + 1) * WIDE)
            if low < high:
                rows = modes_ref[h * half + k].astype(F32)[low - off : high - off]
                stage_ref[(h - g) * WIDE + low : (h - g) * WIDE + high, :] = rows


def synth_y(g, stage_ref, table_ref, work_ref):
    def columns(h, carry):
        lines = dot_nt(table_ref[...], stage_ref[pl.ds(pl.multiple_of(h * WIDE, WIDE), WIDE), :].astype(BF16))
        work_ref[2 * h + g, 0 : lines.shape[0], :] = lines
        return carry

    lax.fori_loop(0, HALVES, columns, 0)


def pack_chunks(work_ref, chunk_ref, g):
    rows = DEVICES * PLANES

    def pack(i, carry):
        lane = pl.ds(pl.multiple_of(i * TILE, TILE), TILE)
        low = work_ref[g, 0:rows, lane].reshape(rows // 8, 8, TILE)
        high = work_ref[2 + g, 0:rows, lane].reshape(rows // 8, 8, TILE)
        upper = rows_of(low.shape, 1) < 4
        even = jnp.where(upper, low, pltpu.roll(high, 4, 1))
        odd = jnp.where(upper, pltpu.roll(low, 4, 1), high)
        both = jnp.stack([even, odd], axis=1).reshape(DEVICES, 8, TILE)
        chunk_ref[:, :, pl.ds(pl.multiple_of(g * WIDE + i * TILE, TILE), TILE)] = both.astype(BF16)
        return carry

    lax.fori_loop(0, WIDE // TILE, pack, 0)


def unpack_rows(chunk_ref, h, at):
    chunk = chunk_ref[:, :, at].astype(F32)
    width = chunk.shape[2]
    pairs = chunk.reshape(DEVICES // 2, 2, 8, width)
    even, odd = pairs[:, 0], pairs[:, 1]
    upper = rows_of(even.shape, 1) < 4
    if h == 0:
        rows = jnp.where(upper, even, pltpu.roll(odd, 4, 1))
    else:
        rows = jnp.where(upper, pltpu.roll(even, 4, 1), odd)
    return rows.reshape(DEVICES * PLANES, width).astype(BF16)


def tile_of(t):
    return slice(t * TILE, (t + 1) * TILE)


def fill_windows(chunk_ref, lines_ref, ks):
    group = DEVICES // 4
    rows = group * 8
    for k in ks:
        first, shift = divmod(k * WINDOW, TILE)
        for a in range(4):
            own = slice(a * group, (a + 1) * group)
            part = chunk_ref[own, :, tile_of(first)].astype(F32).reshape(rows, TILE)
            if shift + WINDOW > TILE:
                right = chunk_ref[own, :, tile_of(first + 1)].astype(F32).reshape(rows, TILE)
                part = jnp.where(rows_of(part.shape, 1) >= shift, part, right)
            if shift:
                part = pltpu.roll(part, TILE - shift, 1)
            lines_ref[k * rows : (k + 1) * rows, tile_of(a)] = part.astype(BF16)


def synth_z(lines_ref, table_ref, plane_ref, stage_ref, ks):
    low, high = ks[0] * 256, (ks[-1] + 1) * 256
    part = (high - low) // PLANES
    for c in range(NZ // BLOCK):
        points = dot(lines_ref[low:high, :], table_ref[:, c * BLOCK : (c + 1) * BLOCK])
        for t in range(BLOCK // TILE):
            stage_ref[t, 0 : high - low, :] = points[:, tile_of(t)]
            for p in range(PLANES):
                plane_ref[p, low // PLANES : high // PLANES, tile_of(c * (BLOCK // TILE) + t)] = stage_ref[
                    t, pl.ds(p, part, stride=PLANES), :
                ].astype(BF16)


def analyse_z(stream_ref, lines_ref, table_ref, chunk_ref, ks):
    group = DEVICES // 4
    rows = group * 8
    low, high = ks[0] * rows, (ks[-1] + 1) * rows
    for c in range(NZ // TILE):
        lines_ref[low:high, tile_of(c)] = stream_ref[c, low:high, :].astype(BF16)
    for pair in range(2):
        lines = dot(lines_ref[low:high, :], table_ref[:, pair * 2 * TILE : (pair + 1) * 2 * TILE])
        for k in ks:
            first, shift = divmod(BASE + k * WINDOW, TILE)
            for n in range(2):
                own = slice((2 * pair + n) * group, (2 * pair + n + 1) * group)
                moved = lines[k * rows - low : (k + 1) * rows - low, tile_of(n)]
                if not shift:
                    chunk_ref[own, :, tile_of(first)] = moved.reshape(group, 8, TILE).astype(BF16)
                    continue
                moved = pltpu.roll(moved, shift, 1).reshape(group, 8, TILE)
                keep = rows_of(moved.shape, 2) >= shift
                chunk_ref[own, :, tile_of(first)] = jnp.where(
                    keep, moved, chunk_ref[own, :, tile_of(first)].astype(F32)
                ).astype(BF16)
                if shift + WINDOW > TILE:
                    chunk_ref[own, :, tile_of(first + 1)] = moved.astype(BF16)


def keep_lines(stream_ref, lines, p):
    for t in range(NZ // TILE):
        stream_ref[t, pl.ds(p, lines.shape[0], stride=PLANES), :] = lines[:, tile_of(t)]


SPARE = 72
LAST = slice(LANES - TILE, LANES)


def last_out(place, work_ref, table_ref, rows_ref):
    lane = rows_of((1, TILE), 1)
    points = DEVICES * PLANES
    table = table_ref[:, pl.ds(pl.multiple_of(place.a * TILE, TILE), TILE)]
    for h in range(HALVES):
        for k in range(11):
            first, shift = divmod(k * WINDOW, TILE)
            tile = lambda t: work_ref[2 * h + t // 4, points : points + 1, (t % 4) * TILE : (t % 4 + 1) * TILE]
            row = tile(first)
            if shift:
                row = pltpu.roll(jnp.where(lane >= shift, row, tile(first + 1)), TILE - shift, 1)
            rows_ref[SPARE + k : SPARE + k + 1, :] = row
        here = slice(WIDE - TILE, WIDE)
        added = dot_nt(table, rows_ref[...].astype(BF16))
        work_ref[2 * h + 1, 0:points, here] = jnp.where(lane < SPARE, work_ref[2 * h + 1, 0:points, here], added)


def last_in(chunk_ref, points_ref, last_ref):
    group = DEVICES // 4
    total = chunk_ref[0:group, :, LAST].astype(F32)
    for a in range(1, 4):
        total = total + chunk_ref[a * group : (a + 1) * group, :, LAST].astype(F32)
    points_ref[0, 0 : group * 8, :] = total.reshape(group * 8, TILE)
    part = group * HALVES
    lines = [points_ref[0, pl.ds(p, part, stride=PLANES), :] for p in range(PLANES)]
    lane = rows_of((part, TILE), 1)
    for k in range(11):
        rows = jnp.zeros((part, TILE), F32)
        for p in range(PLANES):
            rows = jnp.where(lane == p, lines[p][:, SPARE + k : SPARE + k + 1], rows)
        last_ref[k * part : (k + 1) * part, :] = rows.astype(BF16)


def last_back(lines, points_ref):
    part = lines.shape[0] // 11
    lane = rows_of((part, TILE), 1)
    for p in range(PLANES):
        rows = jnp.zeros((part, TILE), F32)
        for k in range(11):
            rows = jnp.where(lane == k, lines[k * part : (k + 1) * part, p : p + 1], rows)
        points_ref[1, pl.ds(p, part, stride=PLANES), :] = rows


def last_fill(points_ref, chunk_ref):
    group = DEVICES // 4
    rows = points_ref[1, 0 : group * 8, :].reshape(group, 8, TILE)
    keep = rows_of(rows.shape, 2) >= BASE
    for a in range(4):
        own = slice(a * group, (a + 1) * group)
        chunk_ref[own, :, 0:TILE] = jnp.where(keep, chunk_ref[own, :, 0:TILE].astype(F32), rows).astype(BF16)


def last_edge(place, chunk_ref, table_ref, edge_ref):
    table = table_ref[:, pl.ds(pl.multiple_of(place.a * TILE, TILE), TILE)]
    lane = rows_of((1, TILE), 1)
    for h in range(HALVES):
        lines = dot_tn(unpack_rows(chunk_ref, h, slice(0, TILE)), table).astype(BF16).astype(F32)
        for k in range(11):
            first, shift = divmod(BASE + k * WINDOW, TILE)
            moved = lines[k : k + 1]
            if not shift:
                edge_ref[h, 0:1, tile_of(first)] = moved
                continue
            moved = pltpu.roll(moved, shift, 1)
            edge_ref[h, 0:1, tile_of(first)] = jnp.where(lane >= shift, moved, edge_ref[h, 0:1, tile_of(first)])
            if shift + WINDOW > TILE:
                edge_ref[h, 0:1, tile_of(first + 1)] = moved


def wave_squares(place, half_span, half_stream, span_local, stream_local, h, start):
    lane = start - BASE + rows_of((1, WIDE), 1)
    k, j = lane // WINDOW, lane % WINDOW

    def squared(mode, count):
        wave = 2.0 * jnp.where(mode < count, mode, mode - count + 1).astype(F32) / count
        return wave * wave

    stream = squared(place.b * stream_local + h * (stream_local // HALVES) + k, half_stream)
    return squared(place.a * span_local + j, half_span) + stream


def kernel(
    phi_hbm, vel_hbm, points_hbm, synth_zt_hbm, synth_z_hbm, synth_x_hbm, analy_x_hbm, analy_z_hbm, analy_y_hbm, slope_hbm,
    dual_hbm, basis_hbm, rates_ref, out_ref,
    modes_ref, table_y_ref, synth_zt_ref, synth_z_ref, synth_x_ref, analy_x_ref, analy_z_ref, analy_y_ref, slope_ref,
    dual_ref, basis_ref, stage_ref, work_ref, solve_ref, plane_ref, points_ref, lines_ref, stream_ref, rows_ref, last_ref, last_phi_ref,
    edge_ref, eig_ref, both_table, ends_ref,
    phi_send, vel_send, phi_recv, vel_recv, cube_recv, flux_recv,
    table_sems, modes_sem, own_sem, phi_sems, vel_sems, cube_sems, flux_sems,
):
    place = Place()
    cheb = dual_ref.shape[0]
    streams, spans, _ = modes_ref.shape
    rows = cheb - 1

    modes_copy = pltpu.make_async_copy(phi_hbm, modes_ref, modes_sem)
    modes_copy.start()
    moves = {}
    pairs = dict(
        points=(points_hbm, table_y_ref), synth_zt=(synth_zt_hbm, synth_zt_ref), dual=(dual_hbm, dual_ref),
        analy_y=(analy_y_hbm, analy_y_ref), slope=(slope_hbm, slope_ref), basis=(basis_hbm, basis_ref),
        synth_z=(synth_z_hbm, synth_z_ref), synth_x=(synth_x_hbm, synth_x_ref), analy_x=(analy_x_hbm, analy_x_ref),
        analy_z=(analy_z_hbm, analy_z_ref),
    )
    for i, (name, (src, dst)) in enumerate(pairs.items()):
        moves[name] = pltpu.make_async_copy(src, dst, table_sems.at[i])
        moves[name].start()

    barrier = pltpu.get_barrier_semaphore()

    def greet(a, b):
        pl.semaphore_signal(barrier, inc=1, device_id=(a, b), device_id_type=MESH)

    place.each(greet)

    stage_ref[...] = jnp.zeros_like(stage_ref)
    rows_ref[...] = jnp.zeros_like(rows_ref)
    edge_ref[...] = jnp.zeros_like(edge_ref)
    modes_copy.wait()
    stage_modes(modes_ref, stage_ref, 0, 0)
    moves["points"].wait()
    synth_y(0, stage_ref, table_y_ref, work_ref)
    pack_chunks(work_ref, phi_send, 0)
    pl.semaphore_wait(barrier, DEVICES - 1)
    scatter(place, phi_send, phi_recv, phi_sems, own_sem, 0)
    stage_modes(modes_ref, stage_ref, 1, 0)
    synth_y(1, stage_ref, table_y_ref, work_ref)
    moves["synth_zt"].wait()
    last_out(place, work_ref, synth_zt_ref, rows_ref)
    pack_chunks(work_ref, phi_send, 1)
    scatter(place, phi_send, phi_recv, phi_sems, own_sem, 1)

    moves["dual"].wait()
    for g in range(2):
        stage_modes(modes_ref, stage_ref, g, BASE)
        if g == 1:
            vel_copy = pltpu.make_async_copy(vel_hbm, modes_ref, modes_sem)
            vel_copy.start()
        for h in range(HALVES):
            solve_ref[h, :, lanes_of(g)] = dot_nt(dual_ref[...], stage_ref[h * WIDE : (h + 1) * WIDE, :].astype(BF16))

    vel_copy.wait()
    for g in range(2):
        stage_modes(modes_ref, stage_ref, g, 0)
        synth_y(g, stage_ref, table_y_ref, work_ref)
        if g == 1:
            last_out(place, work_ref, synth_zt_ref, rows_ref)
        pack_chunks(work_ref, vel_send, g)
        scatter(place, vel_send, vel_recv, vel_sems, own_sem, g)

    for name in ("analy_y", "slope", "basis"):
        moves[name].wait()
    for n, table in enumerate((analy_y_ref, slope_ref)):
        full = dot(dual_ref[...], table[...])
        table[...] = full.astype(BF16)
        ends_ref[n] = jnp.broadcast_to(full[:, rows:cheb], (cheb, TILE))
    full = dot(dual_ref[...], basis_ref[...])
    both_table[...] = full[:, 0:rows].astype(BF16)
    ends_ref[2] = jnp.broadcast_to(full[:, rows:cheb], (cheb, TILE))
    eig_ref[0:rows, :] = -jnp.transpose(jnp.broadcast_to(rates_ref[:, 0:rows], (TILE, rows)))
    eig_ref[rows:cheb, :] = -jnp.broadcast_to(rates_ref[:, rows:cheb], (1, TILE))

    for name in ("synth_z", "synth_x", "analy_x", "analy_z"):
        moves[name].wait()
    early, late = range(0, 5), range(5, 11)

    def planes_of(send, recv, sems):
        all_chunks(place, send, recv, sems, 0).wait_recv()
        fill_windows(recv, lines_ref, early)
        synth_z(lines_ref, synth_z_ref, plane_ref, points_ref, early)
        all_chunks(place, send, recv, sems, 1).wait_recv()
        fill_windows(recv, lines_ref, late)
        synth_z(lines_ref, synth_z_ref, plane_ref, points_ref, late)
        last_in(recv, points_ref, last_ref)

    def back(send, recv, sems, to, to_sems):
        all_chunks(place, send, recv, sems, 0).wait_send()
        all_chunks(place, send, recv, sems, 1).wait_send()
        analyse_z(stream_ref, lines_ref, analy_z_ref, send, range(0, 6))
        last_fill(points_ref, send)
        scatter(place, send, to, to_sems, own_sem, 0)
        analyse_z(stream_ref, lines_ref, analy_z_ref, send, range(6, 11))
        scatter(place, send, to, to_sems, own_sem, 1)

    planes_of(phi_send, phi_recv, phi_sems)

    def cube_plane(p, carry):
        phi = dot(synth_x_ref[...], plane_ref[p])
        work_ref[p] = phi
        keep_lines(stream_ref, dot(analy_x_ref[...], (phi * phi * phi).astype(BF16)), p)
        return carry

    lax.fori_loop(0, PLANES, cube_plane, 0)
    phi = dot(synth_x_ref[...], last_ref[...])
    last_phi_ref[...] = phi
    last_back(dot(analy_x_ref[...], (phi * phi * phi).astype(BF16)), points_ref)
    back(phi_send, phi_recv, phi_sems, cube_recv, cube_sems)

    planes_of(vel_send, vel_recv, vel_sems)

    def flux_plane(p, carry):
        flux = dot(synth_x_ref[...], plane_ref[p]) * work_ref[p]
        keep_lines(stream_ref, dot(analy_x_ref[...], flux.astype(BF16)), p)
        return carry

    lax.fori_loop(0, PLANES, flux_plane, 0)
    flux = dot(synth_x_ref[...], last_ref[...]) * last_phi_ref[...]
    last_back(dot(analy_x_ref[...], flux.astype(BF16)), points_ref)
    back(vel_send, vel_recv, vel_sems, flux_recv, flux_sems)

    def squares_at(h, start):
        return wave_squares(place, spans * 2, streams * 16, spans, streams, h, start)

    eig = eig_ref[:, 0:1]

    def times_both(vector):
        return dot(both_table[...], vector[0:rows].astype(BF16)) + ends_ref[2, :, 0:1] * vector[rows:cheb]

    for g in range(2):
        all_chunks(place, phi_send, cube_recv, cube_sems, g).wait_recv()
        if g == 0:
            last_edge(place, cube_recv, analy_z_ref, edge_ref)
        for h in range(HALVES):
            at = lanes_of(g)
            phi = solve_ref[h, :, at]
            cube = dot(analy_y_ref[:, 0:rows], unpack_rows(cube_recv, h, at)) + ends_ref[0, :, 0:1] * edge_ref[h, 0:1, at]
            lap = times_both((eig - squares_at(h, g * WIDE)) * (cube - (1.0 + stabilizer) * phi))
            solve_ref[h, :, at] = (phi / time_step + mobility * lap) / (capillary * mobility)
    for g in range(2):
        all_chunks(place, vel_send, flux_recv, flux_sems, g).wait_recv()
        if g == 0:
            last_edge(place, flux_recv, analy_z_ref, edge_ref)
        for h in range(HALVES):
            at = lanes_of(g)
            shifted = eig - squares_at(h, g * WIDE)
            slope = dot(slope_ref[:, 0:rows], unpack_rows(flux_recv, h, at)) + ends_ref[1, :, 0:1] * edge_ref[h, 0:1, at]
            forcing = solve_ref[h, :, at] - 8.0 / (cheb - 1) / (capillary * mobility) * slope
            middle = times_both(forcing / (shifted - screen_low))
            out_ref[h, :, at] = (middle / (shifted - screen_high)).astype(BF16)
    for g in range(2):
        all_chunks(place, phi_send, cube_recv, cube_sems, g).wait_send()
        all_chunks(place, vel_send, flux_recv, flux_sems, g).wait_send()


def finish_kernel(second_ref, basis_ref, out_ref):
    half, spans, _ = out_ref.shape
    for start in range(0, LANES, BLOCK):
        result = lax.dot_general(
            second_ref[0, :, start : start + BLOCK], basis_ref[...], (((0,), (1,)), ((), ())), preferred_element_type=F32
        )
        for k in range(half):
            off = BASE + k * WINDOW
            low, high = max(off, start), min(off + spans, start + BLOCK)
            if low < high:
                out_ref[k, low - off : high - off, :] = result[low - start : high - start]


def per_device(phi_hat, vel_hat, helm_basis, helm_dual, helm_rates):
    span_count = lax.axis_size("nz")
    stream_count = lax.axis_size("nx")
    span_local, stream_local, cheb = phi_hat.shape
    half = stream_local // HALVES
    s_x, a_x = fourier_tables(stream_local * stream_count, NX)
    s_z, a_z = fourier_tables(span_local * span_count, NZ)
    s_y, a_y, d_y = chebyshev_tables(cheb)

    points = np.pad(s_y.T, ((0, -cheb % 8), (0, 0)))
    slope = (d_y.astype(np.float64).T @ a_y.astype(np.float64).T).astype(np.float32).astype(BF)
    order = np.arange(stream_local * stream_count).reshape(stream_count, HALVES, half).transpose(2, 0, 1).reshape(-1)
    synth_x = np.ascontiguousarray(s_x.T[:, order])
    analy_x = np.ascontiguousarray(a_x.T[order])
    synth_z = np.pad(s_z.reshape(span_count, span_local, NZ), ((0, 0), (0, TILE - span_local), (0, 0))).reshape(-1, NZ)
    analy_z = np.pad(a_z.reshape(NZ, span_count, span_local), ((0, 0), (0, 0), (0, TILE - span_local))).reshape(NZ, -1)

    large = [jnp.transpose(phi_hat, (1, 0, 2)), jnp.transpose(vel_hat, (1, 0, 2))]
    tables = (points, np.ascontiguousarray(synth_z.T), synth_z, synth_x, analy_x, analy_z, np.ascontiguousarray(a_y.T), slope)
    large += [jnp.asarray(table) for table in tables] + [helm_dual, helm_basis]
    modes_x = stream_local * stream_count
    chunk = pltpu.VMEM((DEVICES, 8, LANES), BF16)
    sems = pltpu.SemaphoreType.DMA((2, 2))
    second = pl.pallas_call(
        kernel,
        out_shape=jax.ShapeDtypeStruct((HALVES, cheb, LANES), BF16),
        in_specs=[pl.BlockSpec(memory_space=pl.ANY)] * len(large) + [pl.BlockSpec(memory_space=pltpu.VMEM)],
        out_specs=pl.BlockSpec(memory_space=pltpu.VMEM),
        scratch_shapes=[pltpu.VMEM(large[0].shape, BF16)]
        + [pltpu.VMEM(table.shape, BF16) for table in large[2:]]
        + [
            pltpu.VMEM((LANES, cheb), F32),
            pltpu.VMEM((PLANES, NX, NZ), F32),
            pltpu.VMEM((HALVES, cheb, LANES), F32),
            pltpu.VMEM((PLANES, modes_x, NZ), BF16),
            pltpu.VMEM((2, 6 * 256, TILE), F32),
            pltpu.VMEM((11 * 256, NZ), BF16),
            pltpu.VMEM((NZ // TILE, 11 * 256, TILE), F32),
            pltpu.VMEM((TILE, TILE), F32),
            pltpu.VMEM((modes_x, TILE), BF16),
            pltpu.VMEM((NX, TILE), F32),
            pltpu.VMEM((HALVES, 8, LANES), F32),
            pltpu.VMEM((cheb, TILE), F32),
            pltpu.VMEM((cheb, cheb - 1), BF16),
            pltpu.VMEM((3, cheb, TILE), F32),
        ]
        + [chunk] * 6
        + [
            pltpu.SemaphoreType.DMA((len(large) - 2,)), pltpu.SemaphoreType.DMA, pltpu.SemaphoreType.DMA,
            sems, sems, sems, sems,
        ],
        compiler_params=pltpu.CompilerParams(collective_id=0, has_side_effects=True, vmem_limit_bytes=60 << 20),
    )(*large, helm_rates.reshape(1, cheb))
    result = pl.pallas_call(
        finish_kernel,
        out_shape=jax.ShapeDtypeStruct((stream_local, span_local, cheb), F32),
        grid=(HALVES,),
        in_specs=[pl.BlockSpec((1, cheb, LANES), lambda h: (h, 0, 0)), pl.BlockSpec((cheb, cheb), lambda h: (0, 0))],
        out_specs=pl.BlockSpec((half, span_local, cheb), lambda h: (h, 0, 0)),
        compiler_params=pltpu.CompilerParams(vmem_limit_bytes=40 << 20),
    )(second, helm_basis)
    return jnp.transpose(result, (1, 0, 2))


def solution(mesh):
    placed = (P("nz", "nx", None), P("nz", "nx", None), P(), P(), P())
    return jax.shard_map(
        per_device, mesh=mesh, in_specs=placed, out_specs=P("nz", "nx", None), check_vma=False
    )
```

```python
import math

import jax
import jax.numpy as jnp
import ml_dtypes
import numpy as np
from jax import lax
from jax.experimental import pallas as pl
from jax.experimental.pallas import tpu as pltpu
from jax.sharding import PartitionSpec as P

NX = 1024
NZ = 512

mobility = 1.0
capillary = 0.2
screen_low = 4.0
screen_high = 20.0
time_step = 1.0 / (screen_low * screen_high * mobility * capillary)
stabilizer = capillary * (screen_low + screen_high)

PLANES = 4
HALVES = 2
WINDOW = 86
LANES = 1024
TILE = 128
BF = ml_dtypes.bfloat16
F32 = jnp.float32
BF16 = jnp.bfloat16


def fourier_tables(mode_count, point_count):
    half_count = mode_count // 2
    mode_index = np.arange(mode_count)
    wave_index = np.where(mode_index < half_count, mode_index, mode_index - half_count + 1)
    phase_steps = wave_index[:, None] * np.arange(point_count)[None, :] % point_count
    angles = phase_steps * (2.0 * math.pi / point_count)
    basis = np.where((mode_index < half_count)[:, None], np.cos(angles), np.sin(angles))
    factor = math.sqrt(2.0 / mode_count)
    weights = np.where(mode_index == 0, 1.0, 2.0) / (point_count * factor)
    return (
        (factor * basis).astype(np.float32).astype(BF),
        (basis.T * weights[None, :]).astype(np.float32).astype(BF),
    )


def chebyshev_tables(count):
    index = np.arange(count)
    phase_steps = index[:, None] * index[None, :] % (2 * (count - 1))
    cosines = np.cos(phase_steps * (math.pi / (count - 1)))
    factor = math.sqrt(2.0 / count)
    ends = np.where((index == 0) | (index == count - 1), 2.0, 1.0)
    analysis = cosines.T * (2.0 / ((count - 1) * factor)) / (ends[:, None] * ends[None, :])
    upper, lower = index[:, None], index[None, :]
    deriv = np.where((upper > lower) & ((upper + lower) % 2 == 1), 2.0 * upper / ends[None, :], 0.0)
    as_bf = lambda t: t.astype(np.float32).astype(BF)
    return as_bf(factor * cosines), as_bf(analysis), as_bf(deriv)


def dot(left, right):
    return jnp.dot(left, right, preferred_element_type=F32)


def dot_nt(left, right):
    return lax.dot_general(left, right, (((1,), (1,)), ((), ())), preferred_element_type=F32)


def dot_tn(left, right):
    return lax.dot_general(left, right, (((0,), (0,)), ((), ())), preferred_element_type=F32)


def rows_of(shape, axis):
    return lax.broadcasted_iota(jnp.int32, shape, axis)


MESH = pl.DeviceIdType.MESH
DEVICES = 128
BLOCK = 256
WIDE = 512
CUTS = (0, 512, 896, 1024)
BASE = 11


class Place:
    def __init__(self):
        self.a, self.b = lax.axis_index("nz"), lax.axis_index("nx")
        self.me = self.a * 32 + self.b
        self.core = self.a & 1
        self.beside = (self.a, self.b ^ 1)
        self.sign = 1 - 2 * self.core
        y = (self.a >> 1) * 2 + ((self.b >> 2) & 1)
        ys = [(y + self.sign * d) & 3 for d in range(4)]
        self.xs = [(self.b + self.sign * d) & 3 for d in range(4)]
        self.ys = [((d >> 1) * 2, (d & 1) * 4) for d in ys]
        self.z = self.b >> 3

    def each(self, visit):
        def some(j, carry):
            core = self.core ^ (j >> 2)
            z = self.z + self.sign * (j & 3)
            for v in range(4):
                for u in range(4):
                    y_hi, y_lo = self.ys[(u + v) & 3]
                    nz = y_hi + core
                    nx = ((z + self.sign * (3 * u + 2 * v)) & 3) * 8 + y_lo + self.xs[u]
                    if u or v:
                        visit(nz, nx)
                    else:
                        pl.when(j > 0)(lambda nz=nz, nx=nx: visit(nz, nx))
            return carry

        lax.fori_loop(0, 8, some, 0)


def transfer(src, dst, sems, device):
    return pltpu.make_async_remote_copy(
        src_ref=src, dst_ref=dst, send_sem=sems.at[0], recv_sem=sems.at[1], device_id=device, device_id_type=MESH
    )


def lanes_of(g):
    return slice(CUTS[g], CUTS[g + 1])


def scatter(place, src, dst, sems, own_sem, g):
    own = pltpu.make_async_copy(src.at[place.me, :, lanes_of(g)], dst.at[place.me, :, lanes_of(g)], own_sem)
    own.start()

    def send(a, b):
        transfer(src.at[a * 32 + b, :, lanes_of(g)], dst.at[place.me, :, lanes_of(g)], sems.at[g], (a, b)).start()

    place.each(send)
    own.wait()


def all_chunks(place, src, dst, sems, g):
    others = pl.ds(0, DEVICES - 1)
    return transfer(src.at[others, :, lanes_of(g)], dst.at[others, :, lanes_of(g)], sems.at[g], place.beside)


def stage_modes(modes_ref, stage_ref, g, base):
    streams, spans, _ = modes_ref.shape
    half = streams // HALVES
    for h in range(HALVES):
        for k in range(half):
            off = base + k * WINDOW
            low, high = max(off, g * WIDE), min(off + spans, (g + 1) * WIDE)
            if low < high:
                rows = modes_ref[h * half + k].astype(F32)[low - off : high - off]
                stage_ref[(h - g) * WIDE + low : (h - g) * WIDE + high, :] = rows


def synth_y(g, stage_ref, table_ref, work_ref):
    def columns(h, carry):
        lines = dot_nt(table_ref[...], stage_ref[pl.ds(pl.multiple_of(h * WIDE, WIDE), WIDE), :].astype(BF16))
        work_ref[2 * h + g, 0 : lines.shape[0], :] = lines
        return carry

    lax.fori_loop(0, HALVES, columns, 0)


def pack_chunks(work_ref, chunk_ref, g):
    rows = DEVICES * PLANES

    def pack(i, carry):
        lane = pl.ds(pl.multiple_of(i * TILE, TILE), TILE)
        low = work_ref[g, 0:rows, lane].reshape(rows // 8, 8, TILE)
        high = work_ref[2 + g, 0:rows, lane].reshape(rows // 8, 8, TILE)
        upper = rows_of(low.shape, 1) < 4
        even = jnp.where(upper, low, pltpu.roll(high, 4, 1))
        odd = jnp.where(upper, pltpu.roll(low, 4, 1), high)
        both = jnp.stack([even, odd], axis=1).reshape(DEVICES, 8, TILE)
        chunk_ref[:, :, pl.ds(pl.multiple_of(g * WIDE + i * TILE, TILE), TILE)] = both.astype(BF16)
        return carry

    lax.fori_loop(0, WIDE // TILE, pack, 0)


def unpack_rows(chunk_ref, h, at):
    chunk = chunk_ref[:, :, at].astype(F32)
    width = chunk.shape[2]
    pairs = chunk.reshape(DEVICES // 2, 2, 8, width)
    even, odd = pairs[:, 0], pairs[:, 1]
    upper = rows_of(even.shape, 1) < 4
    if h == 0:
        rows = jnp.where(upper, even, pltpu.roll(odd, 4, 1))
    else:
        rows = jnp.where(upper, pltpu.roll(even, 4, 1), odd)
    return rows.reshape(DEVICES * PLANES, width).astype(BF16)


def tile_of(t):
    return slice(t * TILE, (t + 1) * TILE)


def fill_windows(chunk_ref, lines_ref, ks):
    group = DEVICES // 4
    rows = group * 8
    for k in ks:
        first, shift = divmod(k * WINDOW, TILE)
        for a in range(4):
            own = slice(a * group, (a + 1) * group)
            part = chunk_ref[own, :, tile_of(first)].astype(F32).reshape(rows, TILE)
            if shift + WINDOW > TILE:
                right = chunk_ref[own, :, tile_of(first + 1)].astype(F32).reshape(rows, TILE)
                part = jnp.where(rows_of(part.shape, 1) >= shift, part, right)
            if shift:
                part = pltpu.roll(part, TILE - shift, 1)
            lines_ref[k * rows : (k + 1) * rows, tile_of(a)] = part.astype(BF16)


def synth_z(lines_ref, table_ref, plane_ref, stage_ref, ks):
    low, high = ks[0] * 256, (ks[-1] + 1) * 256
    part = (high - low) // PLANES
    for c in range(NZ // BLOCK):
        points = dot(lines_ref[low:high, :], table_ref[:, c * BLOCK : (c + 1) * BLOCK])
        for t in range(BLOCK // TILE):
            stage_ref[t, 0 : high - low, :] = points[:, tile_of(t)]
            for p in range(PLANES):
                plane_ref[p, low // PLANES : high // PLANES, tile_of(c * (BLOCK // TILE) + t)] = stage_ref[
                    t, pl.ds(p, part, stride=PLANES), :
                ].astype(BF16)


def analyse_z(stream_ref, lines_ref, table_ref, chunk_ref, ks):
    group = DEVICES // 4
    rows = group * 8
    low, high = ks[0] * rows, (ks[-1] + 1) * rows
    for c in range(NZ // TILE):
        lines_ref[low:high, tile_of(c)] = stream_ref[c, low:high, :].astype(BF16)
    for pair in range(2):
        lines = dot(lines_ref[low:high, :], table_ref[:, pair * 2 * TILE : (pair + 1) * 2 * TILE])
        for k in ks:
            first, shift = divmod(BASE + k * WINDOW, TILE)
            for n in range(2):
                own = slice((2 * pair + n) * group, (2 * pair + n + 1) * group)
                moved = lines[k * rows - low : (k + 1) * rows - low, tile_of(n)]
                if not shift:
                    chunk_ref[own, :, tile_of(first)] = moved.reshape(group, 8, TILE).astype(BF16)
                    continue
                moved = pltpu.roll(moved, shift, 1).reshape(group, 8, TILE)
                keep = rows_of(moved.shape, 2) >= shift
                chunk_ref[own, :, tile_of(first)] = jnp.where(
                    keep, moved, chunk_ref[own, :, tile_of(first)].astype(F32)
                ).astype(BF16)
                if shift + WINDOW > TILE:
                    chunk_ref[own, :, tile_of(first + 1)] = moved.astype(BF16)


def keep_lines(stream_ref, lines, p):
    for t in range(NZ // TILE):
        stream_ref[t, pl.ds(p, lines.shape[0], stride=PLANES), :] = lines[:, tile_of(t)]


LAST = slice(LANES - TILE, LANES)


def join_last(first_ref, second_ref):
    first, second = first_ref[:, :, LAST].astype(F32), second_ref[:, :, LAST].astype(F32)
    moved = pltpu.roll(second.reshape(DEVICES * 8, TILE), TILE // 2, 1).reshape(second.shape)
    second_ref[:, :, LAST] = jnp.where(rows_of(first.shape, 2) < TILE // 2, first, moved).astype(BF16)


def split_last(first_ref, second_ref):
    both = second_ref[:, :, LAST]
    first_ref[:, :, LAST] = both
    moved = pltpu.roll(both.astype(F32).reshape(DEVICES * 8, TILE), TILE // 2, 1).reshape(both.shape)
    second_ref[:, :, LAST] = moved.astype(BF16)


SPARE = 11 * WINDOW - CUTS[2]


def last_out(place, work_ref, table_ref, rows_ref):
    lane = rows_of((1, TILE), 1)
    points = DEVICES * PLANES
    table = table_ref[:, pl.ds(pl.multiple_of(place.a * TILE, TILE), TILE)]
    for h in range(HALVES):
        for k in range(11):
            first, shift = divmod(k * WINDOW, TILE)
            tile = lambda t: work_ref[2 * h + t // 4, points : points + 1, (t % 4) * TILE : (t % 4 + 1) * TILE]
            row = tile(first)
            if shift:
                row = pltpu.roll(jnp.where(lane >= shift, row, tile(first + 1)), TILE - shift, 1)
            rows_ref[SPARE + k : SPARE + k + 1, :] = row
        here = slice(WIDE - TILE, WIDE)
        added = dot_nt(table, rows_ref[...].astype(BF16))
        work_ref[2 * h + 1, 0:points, here] = jnp.where(lane < SPARE, work_ref[2 * h + 1, 0:points, here], added)


def last_in(chunk_ref, points_ref, last_ref):
    group = DEVICES // 4
    total = chunk_ref[0:group, :, LAST].astype(F32)
    for a in range(1, 4):
        total = total + chunk_ref[a * group : (a + 1) * group, :, LAST].astype(F32)
    points_ref[0, 0 : group * 8, :] = total.reshape(group * 8, TILE)
    part = group * HALVES
    lines = [points_ref[0, pl.ds(p, part, stride=PLANES), :] for p in range(PLANES)]
    lane = rows_of((part, TILE), 1)
    for k in range(11):
        rows = jnp.zeros((part, TILE), F32)
        for p in range(PLANES):
            rows = jnp.where(lane == p, lines[p][:, SPARE + k : SPARE + k + 1], rows)
        last_ref[k * part : (k + 1) * part, :] = rows.astype(BF16)


def last_back(lines, points_ref):
    part = lines.shape[0] // 11
    lane = rows_of((part, TILE), 1)
    for p in range(PLANES):
        rows = jnp.zeros((part, TILE), F32)
        for k in range(11):
            rows = jnp.where(lane == k, lines[k * part : (k + 1) * part, p : p + 1], rows)
        points_ref[1, pl.ds(p, part, stride=PLANES), :] = rows


def last_fill(points_ref, chunk_ref):
    group = DEVICES // 4
    rows = points_ref[1, 0 : group * 8, :].reshape(group, 8, TILE)
    keep = rows_of(rows.shape, 2) >= BASE
    for a in range(4):
        own = slice(a * group, (a + 1) * group)
        chunk_ref[own, :, 0:TILE] = jnp.where(keep, chunk_ref[own, :, 0:TILE].astype(F32), rows).astype(BF16)


def last_edge(place, chunk_ref, table_ref, edge_ref):
    table = table_ref[:, pl.ds(pl.multiple_of(place.a * TILE, TILE), TILE)]
    lane = rows_of((1, TILE), 1)
    for h in range(HALVES):
        lines = dot_tn(unpack_rows(chunk_ref, h, slice(0, TILE)), table).astype(BF16).astype(F32)
        for k in range(11):
            first, shift = divmod(BASE + k * WINDOW, TILE)
            moved = lines[k : k + 1]
            if not shift:
                edge_ref[h, 0:1, tile_of(first)] = moved
                continue
            moved = pltpu.roll(moved, shift, 1)
            edge_ref[h, 0:1, tile_of(first)] = jnp.where(lane >= shift, moved, edge_ref[h, 0:1, tile_of(first)])
            if shift + WINDOW > TILE:
                edge_ref[h, 0:1, tile_of(first + 1)] = moved


def wave_squares(place, half_span, half_stream, span_local, stream_local, h, g):
    lane = CUTS[g] - BASE + rows_of((1, CUTS[g + 1] - CUTS[g]), 1)
    k, j = lane // WINDOW, lane % WINDOW

    def squared(mode, count):
        wave = 2.0 * jnp.where(mode < count, mode, mode - count + 1).astype(F32) / count
        return wave * wave

    stream = squared(place.b * stream_local + h * (stream_local // HALVES) + k, half_stream)
    return squared(place.a * span_local + j, half_span) + stream


def kernel(
    phi_hbm, vel_hbm, points_hbm, synth_zt_hbm, synth_z_hbm, synth_x_hbm, analy_x_hbm, analy_z_hbm, analy_y_hbm, slope_hbm,
    dual_hbm, basis_hbm, rates_ref, out_ref,
    modes_ref, table_y_ref, synth_zt_ref, synth_z_ref, synth_x_ref, analy_x_ref, analy_z_ref, analy_y_ref, slope_ref,
    dual_ref, basis_ref, stage_ref, work_ref, solve_ref, plane_ref, points_ref, lines_ref, stream_ref, rows_ref, last_ref, last_phi_ref,
    cube_edge, flux_edge, eig_ref, both_table, ends_ref,
    phi_send, vel_send, phi_recv, vel_recv, cube_recv, flux_recv,
    table_sems, modes_sem, own_sem, phi_sems, vel_sems, cube_sems, flux_sems,
):
    place = Place()
    cheb = dual_ref.shape[0]
    streams, spans, _ = modes_ref.shape
    rows = cheb - 1

    modes_copy = pltpu.make_async_copy(phi_hbm, modes_ref, modes_sem)
    modes_copy.start()
    moves = {}
    pairs = dict(
        points=(points_hbm, table_y_ref), synth_zt=(synth_zt_hbm, synth_zt_ref), dual=(dual_hbm, dual_ref),
        analy_y=(analy_y_hbm, analy_y_ref), slope=(slope_hbm, slope_ref), basis=(basis_hbm, basis_ref),
        synth_z=(synth_z_hbm, synth_z_ref), synth_x=(synth_x_hbm, synth_x_ref), analy_x=(analy_x_hbm, analy_x_ref),
        analy_z=(analy_z_hbm, analy_z_ref),
    )
    for i, (name, (src, dst)) in enumerate(pairs.items()):
        moves[name] = pltpu.make_async_copy(src, dst, table_sems.at[i])
        moves[name].start()

    barrier = pltpu.get_barrier_semaphore()

    def greet(a, b):
        pl.semaphore_signal(barrier, inc=1, device_id=(a, b), device_id_type=MESH)

    place.each(greet)

    stage_ref[...] = jnp.zeros_like(stage_ref)
    rows_ref[...] = jnp.zeros_like(rows_ref)
    cube_edge[...] = jnp.zeros_like(cube_edge)
    flux_edge[...] = jnp.zeros_like(flux_edge)
    modes_copy.wait()
    stage_modes(modes_ref, stage_ref, 0, 0)
    moves["points"].wait()
    synth_y(0, stage_ref, table_y_ref, work_ref)
    pack_chunks(work_ref, phi_send, 0)
    pl.semaphore_wait(barrier, DEVICES - 1)
    scatter(place, phi_send, phi_recv, phi_sems, own_sem, 0)
    stage_modes(modes_ref, stage_ref, 1, 0)
    synth_y(1, stage_ref, table_y_ref, work_ref)
    moves["synth_zt"].wait()
    last_out(place, work_ref, synth_zt_ref, rows_ref)
    pack_chunks(work_ref, phi_send, 1)
    scatter(place, phi_send, phi_recv, phi_sems, own_sem, 1)

    moves["dual"].wait()
    for g in range(2):
        stage_modes(modes_ref, stage_ref, g, BASE)
        if g == 1:
            vel_copy = pltpu.make_async_copy(vel_hbm, modes_ref, modes_sem)
            vel_copy.start()
        for h in range(HALVES):
            solve_ref[h, :, g * WIDE : (g + 1) * WIDE] = dot_nt(dual_ref[...], stage_ref[h * WIDE : (h + 1) * WIDE, :].astype(BF16))

    vel_copy.wait()
    for g in range(2):
        stage_modes(modes_ref, stage_ref, g, 0)
        synth_y(g, stage_ref, table_y_ref, work_ref)
        if g == 1:
            last_out(place, work_ref, synth_zt_ref, rows_ref)
        pack_chunks(work_ref, vel_send, g)
    join_last(phi_send, vel_send)
    for g in (2, 0, 1):
        scatter(place, vel_send, vel_recv, vel_sems, own_sem, g)

    for name in ("analy_y", "slope", "basis"):
        moves[name].wait()
    for n, table in enumerate((analy_y_ref, slope_ref)):
        full = dot(dual_ref[...], table[...])
        table[...] = full.astype(BF16)
        ends_ref[n] = jnp.broadcast_to(full[:, rows:cheb], (cheb, TILE))
    full = dot(dual_ref[...], basis_ref[...])
    both_table[...] = full[:, 0:rows].astype(BF16)
    ends_ref[2] = jnp.broadcast_to(full[:, rows:cheb], (cheb, TILE))
    eig_ref[0:rows, :] = -jnp.transpose(jnp.broadcast_to(rates_ref[...].reshape(1, cheb)[:, 0:rows], (TILE, rows)))
    eig_ref[rows:cheb, :] = -jnp.broadcast_to(rates_ref[...].reshape(1, cheb)[:, rows:cheb], (1, TILE))

    for name in ("synth_z", "synth_x", "analy_x", "analy_z"):
        moves[name].wait()
    def planes_of(recv, ks):
        fill_windows(recv, lines_ref, ks)
        synth_z(lines_ref, synth_z_ref, plane_ref, points_ref, ks)

    def vel_came(g):
        all_chunks(place, vel_send, vel_recv, vel_sems, g).wait_recv()

    for g, ks in enumerate((range(0, 5), range(5, 10))):
        all_chunks(place, phi_send, phi_recv, phi_sems, g).wait_recv()
        planes_of(phi_recv, ks)
    vel_came(2)
    split_last(phi_recv, vel_recv)
    planes_of(phi_recv, range(10, 11))
    last_in(phi_recv, points_ref, last_ref)

    def cube_plane(p, carry):
        phi = dot(synth_x_ref[...], plane_ref[p])
        work_ref[p] = phi
        keep_lines(stream_ref, dot(analy_x_ref[...], (phi * phi * phi).astype(BF16)), p)
        return carry

    lax.fori_loop(0, PLANES, cube_plane, 0)
    phi = dot(synth_x_ref[...], last_ref[...])
    last_phi_ref[...] = phi
    last_back(dot(analy_x_ref[...], (phi * phi * phi).astype(BF16)), points_ref)
    for g in range(2):
        all_chunks(place, phi_send, phi_recv, phi_sems, g).wait_send()
    analyse_z(stream_ref, lines_ref, analy_z_ref, phi_send, range(0, 6))
    last_fill(points_ref, phi_send)
    scatter(place, phi_send, cube_recv, cube_sems, own_sem, 0)
    analyse_z(stream_ref, lines_ref, analy_z_ref, phi_send, range(6, 11))
    scatter(place, phi_send, cube_recv, cube_sems, own_sem, 1)

    vel_came(0)
    planes_of(vel_recv, range(0, 5))
    vel_came(1)
    planes_of(vel_recv, range(5, 11))
    last_in(vel_recv, points_ref, last_ref)

    def flux_plane(p, carry):
        flux = dot(synth_x_ref[...], plane_ref[p]) * work_ref[p]
        keep_lines(stream_ref, dot(analy_x_ref[...], flux.astype(BF16)), p)
        return carry

    lax.fori_loop(0, PLANES, flux_plane, 0)
    flux = dot(synth_x_ref[...], last_ref[...]) * last_phi_ref[...]
    last_back(dot(analy_x_ref[...], flux.astype(BF16)), points_ref)
    for g in range(3):
        all_chunks(place, vel_send, vel_recv, vel_sems, g).wait_send()
    analyse_z(stream_ref, lines_ref, analy_z_ref, vel_send, range(0, 6))
    last_fill(points_ref, vel_send)
    scatter(place, vel_send, flux_recv, flux_sems, own_sem, 0)
    analyse_z(stream_ref, lines_ref, analy_z_ref, vel_send, range(6, 11))
    join_last(phi_send, vel_send)
    scatter(place, vel_send, flux_recv, flux_sems, own_sem, 2)
    scatter(place, vel_send, flux_recv, flux_sems, own_sem, 1)

    def squares_at(h, g):
        return wave_squares(place, spans * 2, streams * 16, spans, streams, h, g)

    eig = eig_ref[:, 0:1]

    def times_both(vector):
        return dot(both_table[...], vector[0:rows].astype(BF16)) + ends_ref[2, :, 0:1] * vector[rows:cheb]

    def lap(g):
        at = lanes_of(g)
        for h in range(HALVES):
            phi = solve_ref[h, :, at]
            cube = dot(analy_y_ref[:, 0:rows], unpack_rows(cube_recv, h, at)) + ends_ref[0, :, 0:1] * cube_edge[h, 0:1, at]
            part = times_both((eig - squares_at(h, g)) * (cube - (1.0 + stabilizer) * phi))
            solve_ref[h, :, at] = (phi / time_step + mobility * part) / (capillary * mobility)

    def solve(g):
        at = lanes_of(g)
        for h in range(HALVES):
            shifted = eig - squares_at(h, g)
            slope = dot(slope_ref[:, 0:rows], unpack_rows(flux_recv, h, at)) + ends_ref[1, :, 0:1] * flux_edge[h, 0:1, at]
            forcing = solve_ref[h, :, at] - 8.0 / (cheb - 1) / (capillary * mobility) * slope
            middle = times_both(forcing / (shifted - screen_low))
            out_ref[h, :, at] = (middle / (shifted - screen_high)).astype(BF16)

    all_chunks(place, phi_send, cube_recv, cube_sems, 0).wait_recv()
    last_edge(place, cube_recv, analy_z_ref, cube_edge)
    lap(0)
    all_chunks(place, phi_send, cube_recv, cube_sems, 1).wait_recv()
    lap(1)
    all_chunks(place, vel_send, flux_recv, flux_sems, 0).wait_recv()
    last_edge(place, flux_recv, analy_z_ref, flux_edge)
    solve(0)
    all_chunks(place, vel_send, flux_recv, flux_sems, 2).wait_recv()
    split_last(cube_recv, flux_recv)
    lap(2)
    solve(2)
    all_chunks(place, vel_send, flux_recv, flux_sems, 1).wait_recv()
    solve(1)
    for g in range(2):
        all_chunks(place, phi_send, cube_recv, cube_sems, g).wait_send()
    for g in range(3):
        all_chunks(place, vel_send, flux_recv, flux_sems, g).wait_send()


def finish_kernel(second_hbm, basis_hbm, out_hbm, second_ref, basis_ref, out_ref, in_sems, out_sems):
    half, spans = out_ref.shape[0] // HALVES, out_ref.shape[1]
    table = pltpu.make_async_copy(basis_hbm, basis_ref, in_sems.at[HALVES])
    table.start()
    moves = [pltpu.make_async_copy(second_hbm.at[h], second_ref.at[h], in_sems.at[h]) for h in range(HALVES)]
    for move in moves:
        move.start()
    table.wait()
    parts = []
    for h in range(HALVES):
        moves[h].wait()
        for g in range(2):
            start = g * WIDE
            result = lax.dot_general(
                second_ref[h, :, start : start + WIDE], basis_ref[...], (((0,), (1,)), ((), ())), preferred_element_type=F32
            )
            done = []
            for k in range(half):
                off = BASE + k * WINDOW
                low, high = max(off, start), min(off + spans, start + WIDE)
                if low < high:
                    out_ref[h * half + k, low - off : high - off, :] = result[low - start : high - start]
                    if high == off + spans:
                        done.append(h * half + k)
            rows = slice(done[0], done[-1] + 1)
            parts.append(pltpu.make_async_copy(out_ref.at[rows], out_hbm.at[rows], out_sems.at[h * 2 + g]))
            parts[-1].start()
    for part in parts:
        part.wait()


def per_device(phi_hat, vel_hat, helm_basis, helm_dual, helm_rates):
    span_count = lax.axis_size("nz")
    stream_count = lax.axis_size("nx")
    span_local, stream_local, cheb = phi_hat.shape
    half = stream_local // HALVES
    s_x, a_x = fourier_tables(stream_local * stream_count, NX)
    s_z, a_z = fourier_tables(span_local * span_count, NZ)
    s_y, a_y, d_y = chebyshev_tables(cheb)

    points = np.pad(s_y.T, ((0, -cheb % 8), (0, 0)))
    slope = (d_y.astype(np.float64).T @ a_y.astype(np.float64).T).astype(np.float32).astype(BF)
    order = np.arange(stream_local * stream_count).reshape(stream_count, HALVES, half).transpose(2, 0, 1).reshape(-1)
    synth_x = np.ascontiguousarray(s_x.T[:, order])
    analy_x = np.ascontiguousarray(a_x.T[order])
    synth_z = np.pad(s_z.reshape(span_count, span_local, NZ), ((0, 0), (0, TILE - span_local), (0, 0))).reshape(-1, NZ)
    analy_z = np.pad(a_z.reshape(NZ, span_count, span_local), ((0, 0), (0, 0), (0, TILE - span_local))).reshape(NZ, -1)

    large = [jnp.transpose(phi_hat, (1, 0, 2)), jnp.transpose(vel_hat, (1, 0, 2))]
    tables = (points, np.ascontiguousarray(synth_z.T), synth_z, synth_x, analy_x, analy_z, np.ascontiguousarray(a_y.T), slope)
    large += [jnp.asarray(table) for table in tables] + [helm_dual, helm_basis]
    modes_x = stream_local * stream_count
    chunk = pltpu.VMEM((DEVICES, 8, LANES), BF16)
    two, three = pltpu.SemaphoreType.DMA((2, 2)), pltpu.SemaphoreType.DMA((3, 2))
    second = pl.pallas_call(
        kernel,
        out_shape=jax.ShapeDtypeStruct((HALVES, cheb, LANES), BF16),
        in_specs=[pl.BlockSpec(memory_space=pl.ANY)] * len(large) + [pl.BlockSpec(memory_space=pltpu.VMEM)],
        out_specs=pl.BlockSpec(memory_space=pltpu.VMEM),
        scratch_shapes=[pltpu.VMEM(large[0].shape, BF16)]
        + [pltpu.VMEM(table.shape, BF16) for table in large[2:]]
        + [
            pltpu.VMEM((LANES, cheb), F32),
            pltpu.VMEM((PLANES, NX, NZ), F32),
            pltpu.VMEM((HALVES, cheb, LANES), F32),
            pltpu.VMEM((PLANES, modes_x, NZ), BF16),
            pltpu.VMEM((2, 6 * 256, TILE), F32),
            pltpu.VMEM((11 * 256, NZ), BF16),
            pltpu.VMEM((NZ // TILE, 11 * 256, TILE), F32),
            pltpu.VMEM((TILE, TILE), F32),
            pltpu.VMEM((modes_x, TILE), BF16),
            pltpu.VMEM((NX, TILE), F32),
            pltpu.VMEM((HALVES, 8, LANES), F32),
            pltpu.VMEM((HALVES, 8, LANES), F32),
            pltpu.VMEM((cheb, TILE), F32),
            pltpu.VMEM((cheb, cheb - 1), BF16),
            pltpu.VMEM((3, cheb, TILE), F32),
        ]
        + [chunk] * 6
        + [
            pltpu.SemaphoreType.DMA((len(large) - 2,)), pltpu.SemaphoreType.DMA, pltpu.SemaphoreType.DMA,
            two, three, two, three,
        ],
        compiler_params=pltpu.CompilerParams(collective_id=0, has_side_effects=True, vmem_limit_bytes=60 << 20),
    )(*large, helm_rates)
    shape = (stream_local, span_local, cheb)
    result = pl.pallas_call(
        finish_kernel,
        out_shape=jax.ShapeDtypeStruct(shape, F32),
        in_specs=[pl.BlockSpec(memory_space=pl.ANY)] * 2,
        out_specs=pl.BlockSpec(memory_space=pl.ANY),
        scratch_shapes=[
            pltpu.VMEM((HALVES, cheb, LANES), BF16), pltpu.VMEM((cheb, cheb), BF16), pltpu.VMEM(shape, F32),
            pltpu.SemaphoreType.DMA((HALVES + 1,)), pltpu.SemaphoreType.DMA((HALVES * 2,)),
        ],
        compiler_params=pltpu.CompilerParams(vmem_limit_bytes=60 << 20),
    )(second, helm_basis)
    return jnp.transpose(result, (1, 0, 2))


def solution(mesh):
    placed = (P("nz", "nx", None), P("nz", "nx", None), P(), P(), P())
    return jax.shard_map(
        per_device, mesh=mesh, in_specs=placed, out_specs=P("nz", "nx", None), check_vma=False
    )
```

```python
import math

import jax
import jax.numpy as jnp
import ml_dtypes
import numpy as np
from jax import lax
from jax.experimental import pallas as pl
from jax.experimental.pallas import tpu as pltpu
from jax.sharding import PartitionSpec as P

NX = 1024
NZ = 512

mobility = 1.0
capillary = 0.2
screen_low = 4.0
screen_high = 20.0
time_step = 1.0 / (screen_low * screen_high * mobility * capillary)
stabilizer = capillary * (screen_low + screen_high)

PLANES = 4
HALVES = 2
WINDOW = 86
LANES = 1024
TILE = 128
BF = ml_dtypes.bfloat16
F32 = jnp.float32
BF16 = jnp.bfloat16


def fourier_tables(mode_count, point_count):
    half_count = mode_count // 2
    mode_index = np.arange(mode_count)
    wave_index = np.where(mode_index < half_count, mode_index, mode_index - half_count + 1)
    phase_steps = wave_index[:, None] * np.arange(point_count)[None, :] % point_count
    angles = phase_steps * (2.0 * math.pi / point_count)
    basis = np.where((mode_index < half_count)[:, None], np.cos(angles), np.sin(angles))
    factor = math.sqrt(2.0 / mode_count)
    weights = np.where(mode_index == 0, 1.0, 2.0) / (point_count * factor)
    return (
        (factor * basis).astype(np.float32).astype(BF),
        (basis.T * weights[None, :]).astype(np.float32).astype(BF),
    )


def chebyshev_tables(count):
    index = np.arange(count)
    phase_steps = index[:, None] * index[None, :] % (2 * (count - 1))
    cosines = np.cos(phase_steps * (math.pi / (count - 1)))
    factor = math.sqrt(2.0 / count)
    ends = np.where((index == 0) | (index == count - 1), 2.0, 1.0)
    analysis = cosines.T * (2.0 / ((count - 1) * factor)) / (ends[:, None] * ends[None, :])
    upper, lower = index[:, None], index[None, :]
    deriv = np.where((upper > lower) & ((upper + lower) % 2 == 1), 2.0 * upper / ends[None, :], 0.0)
    as_bf = lambda t: t.astype(np.float32).astype(BF)
    return as_bf(factor * cosines), as_bf(analysis), as_bf(deriv)


def dot(left, right):
    return jnp.dot(left, right, preferred_element_type=F32)


def dot_nt(left, right):
    return lax.dot_general(left, right, (((1,), (1,)), ((), ())), preferred_element_type=F32)


def dot_tn(left, right):
    return lax.dot_general(left, right, (((0,), (0,)), ((), ())), preferred_element_type=F32)


def rows_of(shape, axis):
    return lax.broadcasted_iota(jnp.int32, shape, axis)


MESH = pl.DeviceIdType.MESH
DEVICES = 128
BLOCK = 256
WIDE = 512
CUTS = (0, 512, 896, 1024)
BASE = 11


class Place:
    def __init__(self):
        self.a, self.b = lax.axis_index("nz"), lax.axis_index("nx")
        self.me = self.a * 32 + self.b
        self.core = self.a & 1
        self.beside = (self.a, self.b ^ 1)
        self.sign = 1 - 2 * self.core
        y = (self.a >> 1) * 2 + ((self.b >> 2) & 1)
        ys = [(y + self.sign * d) & 3 for d in range(4)]
        self.xs = [(self.b + self.sign * d) & 3 for d in range(4)]
        self.ys = [((d >> 1) * 2, (d & 1) * 4) for d in ys]
        self.z = self.b >> 3

    def each(self, visit):
        def some(j, carry):
            core = self.core ^ (j >> 2)
            z = self.z + self.sign * (j & 3)
            for v in range(4):
                for u in range(4):
                    y_hi, y_lo = self.ys[(u + v) & 3]
                    nz = y_hi + core
                    nx = ((z + self.sign * (3 * u + 2 * v)) & 3) * 8 + y_lo + self.xs[u]
                    if u or v:
                        visit(nz, nx)
                    else:
                        pl.when(j > 0)(lambda nz=nz, nx=nx: visit(nz, nx))
            return carry

        lax.fori_loop(0, 8, some, 0)


def transfer(src, dst, sems, device):
    return pltpu.make_async_remote_copy(
        src_ref=src, dst_ref=dst, send_sem=sems.at[0], recv_sem=sems.at[1], device_id=device, device_id_type=MESH
    )


def lanes_of(g):
    return slice(CUTS[g], CUTS[g + 1])


def scatter(place, src, dst, sems, own_sem, g):
    own = pltpu.make_async_copy(src.at[place.me, :, lanes_of(g)], dst.at[place.me, :, lanes_of(g)], own_sem)
    own.start()

    def send(a, b):
        transfer(src.at[a * 32 + b, :, lanes_of(g)], dst.at[place.me, :, lanes_of(g)], sems.at[g], (a, b)).start()

    place.each(send)
    own.wait()


def all_chunks(place, src, dst, sems, g):
    others = pl.ds(0, DEVICES - 1)
    return transfer(src.at[others, :, lanes_of(g)], dst.at[others, :, lanes_of(g)], sems.at[g], place.beside)


def stage_modes(modes_ref, stage_ref, g, base):
    streams, spans, _ = modes_ref.shape
    half = streams // HALVES
    for h in range(HALVES):
        for k in range(half):
            off = base + k * WINDOW
            low, high = max(off, g * WIDE), min(off + spans, (g + 1) * WIDE)
            if low < high:
                rows = modes_ref[h * half + k].astype(F32)[low - off : high - off]
                stage_ref[(h - g) * WIDE + low : (h - g) * WIDE + high, :] = rows


def synth_y(g, stage_ref, table_ref, work_ref):
    def columns(h, carry):
        lines = dot_nt(table_ref[...], stage_ref[pl.ds(pl.multiple_of(h * WIDE, WIDE), WIDE), :].astype(BF16))
        work_ref[2 * h + g, 0 : lines.shape[0], :] = lines
        return carry

    lax.fori_loop(0, HALVES, columns, 0)


def pack_chunks(work_ref, chunk_ref, g):
    rows = DEVICES * PLANES

    def pack(i, carry):
        lane = pl.ds(pl.multiple_of(i * TILE, TILE), TILE)
        low = work_ref[g, 0:rows, lane].reshape(rows // 8, 8, TILE)
        high = work_ref[2 + g, 0:rows, lane].reshape(rows // 8, 8, TILE)
        upper = rows_of(low.shape, 1) < 4
        even = jnp.where(upper, low, pltpu.roll(high, 4, 1))
        odd = jnp.where(upper, pltpu.roll(low, 4, 1), high)
        both = jnp.stack([even, odd], axis=1).reshape(DEVICES, 8, TILE)
        chunk_ref[:, :, pl.ds(pl.multiple_of(g * WIDE + i * TILE, TILE), TILE)] = both.astype(BF16)
        return carry

    lax.fori_loop(0, WIDE // TILE, pack, 0)


def unpack_rows(chunk_ref, h, at):
    chunk = chunk_ref[:, :, at].astype(F32)
    width = chunk.shape[2]
    pairs = chunk.reshape(DEVICES // 2, 2, 8, width)
    even, odd = pairs[:, 0], pairs[:, 1]
    upper = rows_of(even.shape, 1) < 4
    if h == 0:
        rows = jnp.where(upper, even, pltpu.roll(odd, 4, 1))
    else:
        rows = jnp.where(upper, pltpu.roll(even, 4, 1), odd)
    return rows.reshape(DEVICES * PLANES, width).astype(BF16)


def tile_of(t):
    return slice(t * TILE, (t + 1) * TILE)


def fill_windows(chunk_ref, lines_ref, ks):
    group = DEVICES // 4
    rows = group * 8
    for k in ks:
        first, shift = divmod(k * WINDOW, TILE)
        for a in range(4):
            own = slice(a * group, (a + 1) * group)
            part = chunk_ref[own, :, tile_of(first)].astype(F32).reshape(rows, TILE)
            if shift + WINDOW > TILE:
                right = chunk_ref[own, :, tile_of(first + 1)].astype(F32).reshape(rows, TILE)
                part = jnp.where(rows_of(part.shape, 1) >= shift, part, right)
            if shift:
                part = pltpu.roll(part, TILE - shift, 1)
            lines_ref[k * rows : (k + 1) * rows, tile_of(a)] = part.astype(BF16)


def synth_z(lines_ref, table_ref, plane_ref, stage_ref, ks):
    low, high = ks[0] * 256, (ks[-1] + 1) * 256
    part = (high - low) // PLANES
    for c in range(NZ // BLOCK):
        points = dot(lines_ref[low:high, :], table_ref[:, c * BLOCK : (c + 1) * BLOCK])
        for t in range(BLOCK // TILE):
            stage_ref[t, 0 : high - low, :] = points[:, tile_of(t)]
            for p in range(PLANES):
                plane_ref[p, low // PLANES : high // PLANES, tile_of(c * (BLOCK // TILE) + t)] = stage_ref[
                    t, pl.ds(p, part, stride=PLANES), :
                ].astype(BF16)


def analyse_z(stream_ref, lines_ref, table_ref, chunk_ref, ks):
    group = DEVICES // 4
    rows = group * 8
    low, high = ks[0] * rows, (ks[-1] + 1) * rows
    for c in range(NZ // TILE):
        lines_ref[low:high, tile_of(c)] = stream_ref[c, low:high, :].astype(BF16)
    for pair in range(2):
        lines = dot(lines_ref[low:high, :], table_ref[:, pair * 2 * TILE : (pair + 1) * 2 * TILE])
        for k in ks:
            first, shift = divmod(BASE + k * WINDOW, TILE)
            for n in range(2):
                own = slice((2 * pair + n) * group, (2 * pair + n + 1) * group)
                moved = lines[k * rows - low : (k + 1) * rows - low, tile_of(n)]
                if not shift:
                    chunk_ref[own, :, tile_of(first)] = moved.reshape(group, 8, TILE).astype(BF16)
                    continue
                moved = pltpu.roll(moved, shift, 1).reshape(group, 8, TILE)
                keep = rows_of(moved.shape, 2) >= shift
                chunk_ref[own, :, tile_of(first)] = jnp.where(
                    keep, moved, chunk_ref[own, :, tile_of(first)].astype(F32)
                ).astype(BF16)
                if shift + WINDOW > TILE:
                    chunk_ref[own, :, tile_of(first + 1)] = moved.astype(BF16)


def keep_lines(stream_ref, lines, p):
    for t in range(NZ // TILE):
        stream_ref[t, pl.ds(p, lines.shape[0], stride=PLANES), :] = lines[:, tile_of(t)]


LAST = slice(LANES - TILE, LANES)


def join_last(first_ref, second_ref):
    first, second = first_ref[:, :, LAST].astype(F32), second_ref[:, :, LAST].astype(F32)
    moved = pltpu.roll(second.reshape(DEVICES * 8, TILE), TILE // 2, 1).reshape(second.shape)
    second_ref[:, :, LAST] = jnp.where(rows_of(first.shape, 2) < TILE // 2, first, moved).astype(BF16)


def split_last(first_ref, second_ref):
    both = second_ref[:, :, LAST]
    first_ref[:, :, LAST] = both
    moved = pltpu.roll(both.astype(F32).reshape(DEVICES * 8, TILE), TILE // 2, 1).reshape(both.shape)
    second_ref[:, :, LAST] = moved.astype(BF16)


SPARE = 11 * WINDOW - CUTS[2]


def last_out(place, work_ref, table_ref, rows_ref):
    lane = rows_of((1, TILE), 1)
    points = DEVICES * PLANES
    table = table_ref[:, pl.ds(pl.multiple_of(place.a * TILE, TILE), TILE)]
    for h in range(HALVES):
        for k in range(11):
            first, shift = divmod(k * WINDOW, TILE)
            tile = lambda t: work_ref[2 * h + t // 4, points : points + 1, (t % 4) * TILE : (t % 4 + 1) * TILE]
            row = tile(first)
            if shift:
                row = pltpu.roll(jnp.where(lane >= shift, row, tile(first + 1)), TILE - shift, 1)
            rows_ref[SPARE + k : SPARE + k + 1, :] = row
        here = slice(WIDE - TILE, WIDE)
        added = dot_nt(table, rows_ref[...].astype(BF16))
        work_ref[2 * h + 1, 0:points, here] = jnp.where(lane < SPARE, work_ref[2 * h + 1, 0:points, here], added)


def last_in(chunk_ref, points_ref, last_ref):
    group = DEVICES // 4
    total = chunk_ref[0:group, :, LAST].astype(F32)
    for a in range(1, 4):
        total = total + chunk_ref[a * group : (a + 1) * group, :, LAST].astype(F32)
    points_ref[0, 0 : group * 8, :] = total.reshape(group * 8, TILE)
    part = group * HALVES
    lines = [points_ref[0, pl.ds(p, part, stride=PLANES), :] for p in range(PLANES)]
    lane = rows_of((part, TILE), 1)
    for k in range(11):
        rows = jnp.zeros((part, TILE), F32)
        for p in range(PLANES):
            rows = jnp.where(lane == p, lines[p][:, SPARE + k : SPARE + k + 1], rows)
        last_ref[k * part : (k + 1) * part, :] = rows.astype(BF16)


def last_back(lines, points_ref):
    part = lines.shape[0] // 11
    lane = rows_of((part, TILE), 1)
    for p in range(PLANES):
        rows = jnp.zeros((part, TILE), F32)
        for k in range(11):
            rows = jnp.where(lane == k, lines[k * part : (k + 1) * part, p : p + 1], rows)
        points_ref[1, pl.ds(p, part, stride=PLANES), :] = rows


def last_fill(points_ref, chunk_ref):
    group = DEVICES // 4
    rows = points_ref[1, 0 : group * 8, :].reshape(group, 8, TILE)
    keep = rows_of(rows.shape, 2) >= BASE
    for a in range(4):
        own = slice(a * group, (a + 1) * group)
        chunk_ref[own, :, 0:TILE] = jnp.where(keep, chunk_ref[own, :, 0:TILE].astype(F32), rows).astype(BF16)


def last_edge(place, chunk_ref, table_ref, edge_ref):
    table = table_ref[:, pl.ds(pl.multiple_of(place.a * TILE, TILE), TILE)]
    lane = rows_of((1, TILE), 1)
    for h in range(HALVES):
        lines = dot_tn(unpack_rows(chunk_ref, h, slice(0, TILE)), table).astype(BF16).astype(F32)
        for k in range(11):
            first, shift = divmod(BASE + k * WINDOW, TILE)
            moved = lines[k : k + 1]
            if not shift:
                edge_ref[h, 0:1, tile_of(first)] = moved
                continue
            moved = pltpu.roll(moved, shift, 1)
            edge_ref[h, 0:1, tile_of(first)] = jnp.where(lane >= shift, moved, edge_ref[h, 0:1, tile_of(first)])
            if shift + WINDOW > TILE:
                edge_ref[h, 0:1, tile_of(first + 1)] = moved


def wave_squares(place, half_span, half_stream, span_local, stream_local, h, g):
    lane = CUTS[g] - BASE + rows_of((1, CUTS[g + 1] - CUTS[g]), 1)
    k, j = lane // WINDOW, lane % WINDOW

    def squared(mode, count):
        wave = 2.0 * jnp.where(mode < count, mode, mode - count + 1).astype(F32) / count
        return wave * wave

    stream = squared(place.b * stream_local + h * (stream_local // HALVES) + k, half_stream)
    return squared(place.a * span_local + j, half_span) + stream


def kernel(
    phi_hbm, vel_hbm, points_hbm, synth_zt_hbm, synth_z_hbm, synth_x_hbm, analy_x_hbm, analy_z_hbm, analy_y_hbm, slope_hbm,
    dual_hbm, basis_hbm, rates_ref, out_ref,
    modes_ref, table_y_ref, synth_zt_ref, synth_z_ref, synth_x_ref, analy_x_ref, analy_z_ref, analy_y_ref, slope_ref,
    dual_ref, basis_ref, stage_ref, work_ref, solve_ref, plane_ref, points_ref, lines_ref, stream_ref, rows_ref, last_ref, last_phi_ref,
    cube_edge, flux_edge, eig_ref, both_table, ends_ref,
    phi_send, vel_send, phi_recv, vel_recv, cube_recv, flux_recv,
    table_sems, modes_sem, own_sem, phi_sems, vel_sems, cube_sems, flux_sems,
):
    place = Place()
    cheb = dual_ref.shape[0]
    streams, spans, _ = modes_ref.shape
    rows = cheb - 1

    modes_copy = pltpu.make_async_copy(phi_hbm, modes_ref, modes_sem)
    modes_copy.start()
    moves = {}
    pairs = dict(
        points=(points_hbm, table_y_ref), synth_zt=(synth_zt_hbm, synth_zt_ref), dual=(dual_hbm, dual_ref),
        analy_y=(analy_y_hbm, analy_y_ref), slope=(slope_hbm, slope_ref), basis=(basis_hbm, basis_ref),
        synth_z=(synth_z_hbm, synth_z_ref), synth_x=(synth_x_hbm, synth_x_ref), analy_x=(analy_x_hbm, analy_x_ref),
        analy_z=(analy_z_hbm, analy_z_ref),
    )
    for i, (name, (src, dst)) in enumerate(pairs.items()):
        moves[name] = pltpu.make_async_copy(src, dst, table_sems.at[i])
        moves[name].start()

    barrier = pltpu.get_barrier_semaphore()

    def greet(a, b):
        pl.semaphore_signal(barrier, inc=1, device_id=(a, b), device_id_type=MESH)

    place.each(greet)

    stage_ref[...] = jnp.zeros_like(stage_ref)
    rows_ref[...] = jnp.zeros_like(rows_ref)
    cube_edge[...] = jnp.zeros_like(cube_edge)
    flux_edge[...] = jnp.zeros_like(flux_edge)
    modes_copy.wait()
    stage_modes(modes_ref, stage_ref, 0, 0)
    moves["points"].wait()
    synth_y(0, stage_ref, table_y_ref, work_ref)
    pack_chunks(work_ref, phi_send, 0)
    pl.semaphore_wait(barrier, DEVICES - 1)
    scatter(place, phi_send, phi_recv, phi_sems, own_sem, 0)
    stage_modes(modes_ref, stage_ref, 1, 0)
    synth_y(1, stage_ref, table_y_ref, work_ref)
    moves["synth_zt"].wait()
    last_out(place, work_ref, synth_zt_ref, rows_ref)
    pack_chunks(work_ref, phi_send, 1)
    scatter(place, phi_send, phi_recv, phi_sems, own_sem, 1)

    moves["dual"].wait()
    for g in range(2):
        stage_modes(modes_ref, stage_ref, g, BASE)
        if g == 1:
            vel_copy = pltpu.make_async_copy(vel_hbm, modes_ref, modes_sem)
            vel_copy.start()
        for h in range(HALVES):
            solve_ref[h, :, g * WIDE : (g + 1) * WIDE] = dot_nt(dual_ref[...], stage_ref[h * WIDE : (h + 1) * WIDE, :].astype(BF16))

    vel_copy.wait()
    for g in range(2):
        stage_modes(modes_ref, stage_ref, g, 0)
        synth_y(g, stage_ref, table_y_ref, work_ref)
        if g == 1:
            last_out(place, work_ref, synth_zt_ref, rows_ref)
        pack_chunks(work_ref, vel_send, g)
    join_last(phi_send, vel_send)
    for g in (2, 0, 1):
        scatter(place, vel_send, vel_recv, vel_sems, own_sem, g)

    for name in ("analy_y", "slope", "basis"):
        moves[name].wait()
    for n, table in enumerate((analy_y_ref, slope_ref)):
        full = dot(dual_ref[...], table[...])
        table[...] = full.astype(BF16)
        ends_ref[n] = jnp.broadcast_to(full[:, rows:cheb], (cheb, TILE))
    full = dot(dual_ref[...], basis_ref[...])
    both_table[...] = full[:, 0:rows].astype(BF16)
    ends_ref[2] = jnp.broadcast_to(full[:, rows:cheb], (cheb, TILE))
    eig_ref[0:rows, :] = -jnp.transpose(jnp.broadcast_to(rates_ref[...].reshape(1, cheb)[:, 0:rows], (TILE, rows)))
    eig_ref[rows:cheb, :] = -jnp.broadcast_to(rates_ref[...].reshape(1, cheb)[:, rows:cheb], (1, TILE))

    for name in ("synth_z", "synth_x", "analy_x", "analy_z"):
        moves[name].wait()
    def planes_of(recv, ks):
        fill_windows(recv, lines_ref, ks)
        synth_z(lines_ref, synth_z_ref, plane_ref, points_ref, ks)

    def vel_came(g):
        all_chunks(place, vel_send, vel_recv, vel_sems, g).wait_recv()

    for g, ks in enumerate((range(0, 5), range(5, 10))):
        all_chunks(place, phi_send, phi_recv, phi_sems, g).wait_recv()
        planes_of(phi_recv, ks)
    vel_came(2)
    split_last(phi_recv, vel_recv)
    planes_of(phi_recv, range(10, 11))
    last_in(phi_recv, points_ref, last_ref)

    def cube_plane(p, carry):
        phi = dot(synth_x_ref[...], plane_ref[p])
        work_ref[p] = phi
        keep_lines(stream_ref, dot(analy_x_ref[...], (phi * phi * phi).astype(BF16)), p)
        return carry

    lax.fori_loop(0, PLANES, cube_plane, 0)
    phi = dot(synth_x_ref[...], last_ref[...])
    last_phi_ref[...] = phi
    last_back(dot(analy_x_ref[...], (phi * phi * phi).astype(BF16)), points_ref)
    for g in range(2):
        all_chunks(place, phi_send, phi_recv, phi_sems, g).wait_send()
    analyse_z(stream_ref, lines_ref, analy_z_ref, phi_send, range(0, 6))
    last_fill(points_ref, phi_send)
    scatter(place, phi_send, cube_recv, cube_sems, own_sem, 0)
    analyse_z(stream_ref, lines_ref, analy_z_ref, phi_send, range(6, 11))
    scatter(place, phi_send, cube_recv, cube_sems, own_sem, 1)

    vel_came(0)
    planes_of(vel_recv, range(0, 5))
    vel_came(1)
    planes_of(vel_recv, range(5, 11))
    last_in(vel_recv, points_ref, last_ref)

    def flux_plane(p, carry):
        flux = dot(synth_x_ref[...], plane_ref[p]) * work_ref[p]
        keep_lines(stream_ref, dot(analy_x_ref[...], flux.astype(BF16)), p)
        return carry

    lax.fori_loop(0, PLANES, flux_plane, 0)
    flux = dot(synth_x_ref[...], last_ref[...]) * last_phi_ref[...]
    last_back(dot(analy_x_ref[...], flux.astype(BF16)), points_ref)
    for g in range(3):
        all_chunks(place, vel_send, vel_recv, vel_sems, g).wait_send()
    analyse_z(stream_ref, lines_ref, analy_z_ref, vel_send, range(0, 6))
    last_fill(points_ref, vel_send)
    scatter(place, vel_send, flux_recv, flux_sems, own_sem, 0)
    analyse_z(stream_ref, lines_ref, analy_z_ref, vel_send, range(6, 11))
    join_last(phi_send, vel_send)
    scatter(place, vel_send, flux_recv, flux_sems, own_sem, 2)
    scatter(place, vel_send, flux_recv, flux_sems, own_sem, 1)

    def squares_at(h, g):
        return wave_squares(place, spans * 2, streams * 16, spans, streams, h, g)

    eig = eig_ref[:, 0:1]

    def times_both(vector):
        return dot(both_table[...], vector[0:rows].astype(BF16)) + ends_ref[2, :, 0:1] * vector[rows:cheb]

    def lap(g):
        at = lanes_of(g)
        for h in range(HALVES):
            phi = solve_ref[h, :, at]
            cube = dot(analy_y_ref[:, 0:rows], unpack_rows(cube_recv, h, at)) + ends_ref[0, :, 0:1] * cube_edge[h, 0:1, at]
            part = times_both((eig - squares_at(h, g)) * (cube - (1.0 + stabilizer) * phi))
            solve_ref[h, :, at] = (phi / time_step + mobility * part) / (capillary * mobility)

    def solve(g):
        at = lanes_of(g)
        for h in range(HALVES):
            shifted = eig - squares_at(h, g)
            slope = dot(slope_ref[:, 0:rows], unpack_rows(flux_recv, h, at)) + ends_ref[1, :, 0:1] * flux_edge[h, 0:1, at]
            forcing = solve_ref[h, :, at] - 8.0 / (cheb - 1) / (capillary * mobility) * slope
            middle = times_both(forcing / (shifted - screen_low))
            out_ref[h, :, at] = (middle / (shifted - screen_high)).astype(BF16)

    all_chunks(place, phi_send, cube_recv, cube_sems, 0).wait_recv()
    last_edge(place, cube_recv, analy_z_ref, cube_edge)
    lap(0)
    all_chunks(place, phi_send, cube_recv, cube_sems, 1).wait_recv()
    lap(1)
    all_chunks(place, vel_send, flux_recv, flux_sems, 0).wait_recv()
    last_edge(place, flux_recv, analy_z_ref, flux_edge)
    solve(0)
    all_chunks(place, vel_send, flux_recv, flux_sems, 2).wait_recv()
    split_last(cube_recv, flux_recv)
    lap(2)
    solve(2)
    all_chunks(place, vel_send, flux_recv, flux_sems, 1).wait_recv()
    solve(1)
    for g in range(2):
        all_chunks(place, phi_send, cube_recv, cube_sems, g).wait_send()
    for g in range(3):
        all_chunks(place, vel_send, flux_recv, flux_sems, g).wait_send()


def finish_kernel(second_hbm, basis_hbm, out_hbm, second_ref, basis_ref, out_ref, in_sems, out_sems):
    half, spans = out_ref.shape[0] // HALVES, out_ref.shape[1]
    table = pltpu.make_async_copy(basis_hbm, basis_ref, in_sems.at[HALVES])
    table.start()
    moves = [pltpu.make_async_copy(second_hbm.at[h], second_ref.at[h], in_sems.at[h]) for h in range(HALVES)]
    for move in moves:
        move.start()
    table.wait()
    parts = []
    for h in range(HALVES):
        moves[h].wait()
        for g in range(2):
            start = g * WIDE
            result = lax.dot_general(
                second_ref[h, :, start : start + WIDE], basis_ref[...], (((0,), (1,)), ((), ())), preferred_element_type=F32
            )
            done = []
            for k in range(half):
                off = BASE + k * WINDOW
                low, high = max(off, start), min(off + spans, start + WIDE)
                if low < high:
                    out_ref[h * half + k, low - off : high - off, :] = result[low - start : high - start]
                    if high == off + spans:
                        done.append(h * half + k)
            rows = slice(done[0], done[-1] + 1)
            parts.append(pltpu.make_async_copy(out_ref.at[rows], out_hbm.at[rows], out_sems.at[h * 2 + g]))
            parts[-1].start()
    for part in parts:
        part.wait()


def per_device(phi_hat, vel_hat, helm_basis, helm_dual, helm_rates):
    span_count = lax.axis_size("nz")
    stream_count = lax.axis_size("nx")
    span_local, stream_local, cheb = phi_hat.shape
    half = stream_local // HALVES
    s_x, a_x = fourier_tables(stream_local * stream_count, NX)
    s_z, a_z = fourier_tables(span_local * span_count, NZ)
    s_y, a_y, d_y = chebyshev_tables(cheb)

    points = np.pad(s_y.T, ((0, -cheb % 8), (0, 0)))
    slope = (d_y.astype(np.float64).T @ a_y.astype(np.float64).T).astype(np.float32).astype(BF)
    order = np.arange(stream_local * stream_count).reshape(stream_count, HALVES, half).transpose(2, 0, 1).reshape(-1)
    synth_x = np.ascontiguousarray(s_x.T[:, order])
    analy_x = np.ascontiguousarray(a_x.T[order])
    synth_z = np.pad(s_z.reshape(span_count, span_local, NZ), ((0, 0), (0, TILE - span_local), (0, 0))).reshape(-1, NZ)
    analy_z = np.pad(a_z.reshape(NZ, span_count, span_local), ((0, 0), (0, 0), (0, TILE - span_local))).reshape(NZ, -1)

    large = [jnp.transpose(phi_hat, (1, 0, 2)), jnp.transpose(vel_hat, (1, 0, 2))]
    tables = (points, np.ascontiguousarray(synth_z.T), synth_z, synth_x, analy_x, analy_z, np.ascontiguousarray(a_y.T), slope)
    large += [jnp.asarray(table) for table in tables] + [helm_dual, helm_basis]
    modes_x = stream_local * stream_count
    chunk = pltpu.VMEM((DEVICES, 8, LANES), BF16)
    two, three = pltpu.SemaphoreType.DMA((2, 2)), pltpu.SemaphoreType.DMA((3, 2))
    second = pl.pallas_call(
        kernel,
        out_shape=jax.ShapeDtypeStruct((HALVES, cheb, LANES), BF16),
        in_specs=[pl.BlockSpec(memory_space=pl.ANY)] * len(large) + [pl.BlockSpec(memory_space=pltpu.VMEM)],
        out_specs=pl.BlockSpec(memory_space=pltpu.VMEM),
        scratch_shapes=[pltpu.VMEM(large[0].shape, BF16)]
        + [pltpu.VMEM(table.shape, BF16) for table in large[2:]]
        + [
            pltpu.VMEM((LANES + 16, cheb), F32),
            pltpu.VMEM((PLANES, NX, NZ), F32),
            pltpu.VMEM((HALVES, cheb, LANES), F32),
            pltpu.VMEM((PLANES, modes_x, NZ), BF16),
            pltpu.VMEM((2, 6 * 256, TILE), F32),
            pltpu.VMEM((11 * 256, NZ), BF16),
            pltpu.VMEM((NZ // TILE, 11 * 256, TILE), F32),
            pltpu.VMEM((TILE, TILE), F32),
            pltpu.VMEM((modes_x, TILE), BF16),
            pltpu.VMEM((NX, TILE), F32),
            pltpu.VMEM((HALVES, 8, LANES), F32),
            pltpu.VMEM((HALVES, 8, LANES), F32),
            pltpu.VMEM((cheb, TILE), F32),
            pltpu.VMEM((cheb, cheb - 1), BF16),
            pltpu.VMEM((3, cheb, TILE), F32),
        ]
        + [chunk] * 6
        + [
            pltpu.SemaphoreType.DMA((len(large) - 2,)), pltpu.SemaphoreType.DMA, pltpu.SemaphoreType.DMA,
            two, three, two, three,
        ],
        compiler_params=pltpu.CompilerParams(collective_id=0, has_side_effects=True, vmem_limit_bytes=60 << 20),
    )(*large, helm_rates)
    shape = (stream_local, span_local, cheb)
    result = pl.pallas_call(
        finish_kernel,
        out_shape=jax.ShapeDtypeStruct(shape, F32),
        in_specs=[pl.BlockSpec(memory_space=pl.ANY)] * 2,
        out_specs=pl.BlockSpec(memory_space=pl.ANY),
        scratch_shapes=[
            pltpu.VMEM((HALVES, cheb, LANES), BF16), pltpu.VMEM((cheb, cheb), BF16), pltpu.VMEM(shape, F32),
            pltpu.SemaphoreType.DMA((HALVES + 1,)), pltpu.SemaphoreType.DMA((HALVES * 2,)),
        ],
        compiler_params=pltpu.CompilerParams(vmem_limit_bytes=60 << 20),
    )(second, helm_basis)
    return jnp.transpose(result, (1, 0, 2))


def solution(mesh):
    placed = (P("nz", "nx", None), P("nz", "nx", None), P(), P(), P())
    return jax.shard_map(
        per_device, mesh=mesh, in_specs=placed, out_specs=P("nz", "nx", None), check_vma=False
    )
```
